32 devices in a mesh: group: 4 (over y, x), replica: 8 (over z, core).
Axes of the slice: x: 2, y: 2, z: 4, core: 2. Of those that a mesh axis runs over, the one named last changes fastest.
Arguments:
- tokens: bfloat16 [8, 512, 2048], P('replica', 'group'), may hold values from -6 to 6
- seq_lengths: int32 [8, 5], P('replica'), may hold values from 1 to 384, as said below
- attn_gain: bfloat16 [2048], P('group'), may hold values from 0.5 to 1.5
- w_query: bfloat16 [2048, 2048], P('group'), may hold values from -0.125 to 0.125
- w_key: bfloat16 [2048, 512], P('group'), may hold values from -0.125 to 0.125
- w_value: bfloat16 [2048, 512], P('group'), may hold values from -0.125 to 0.125
- w_out: bfloat16 [2048, 2048], P('group'), may hold values from -0.5 to 0.5
- mlp_gain: bfloat16 [2048], P('group'), may hold values from 0.5 to 1.5
- w_gate: bfloat16 [2048, 8192], P('group'), may hold values from -0.125 to 0.125
- w_up: bfloat16 [2048, 8192], P('group'), may hold values from -0.125 to 0.125
- w_down: bfloat16 [8192, 2048], P('group'), may hold values from -0.125 to 0.125
- cotangent: bfloat16 [8, 512, 2048], P('replica', 'group'), may hold values from -6 to 6
Outputs:
- output: bfloat16 [8, 512, 2048], P('replica', 'group')
- grad_tokens: bfloat16 [8, 512, 2048], P('replica', 'group')
- grad_attn_gain: float32 [2048], P('group')
- grad_query: float32 [2048, 2048], P('group')
- grad_key: float32 [2048, 512], P('group')
- grad_value: float32 [2048, 512], P('group')
- grad_out: float32 [2048, 2048], P('group')
- grad_mlp_gain: float32 [2048], P('group')
- grad_gate: float32 [2048, 8192], P('group')
- grad_up: float32 [2048, 8192], P('group')
- grad_down: float32 [8192, 2048], P('group')
The draws below stay inside these ranges and needn't reach their ends.
Inputs may be any that keep to these rules, and one draw needn't show every extreme that they name: `seq_lengths`: each row holds a prompt length from 256 to 384 followed by 4 continuation lengths of one or more; a row sums to 512; in some row the prompt has exactly 384 tokens.
All inputs are finite; a program needn't handle non-finite values.
Results may differ from the reference program's by a relative error of at most 0.024.
Values may be sent and summed in bfloat16 or wider, within the bound.
No kernel may reach another device: no remote copies, remote signals or barrier semaphores. Data moves between devices by JAX's collectives and lax.ppermute only.
A program may use at most 384 MiB of HBM per device.

```python
import jax
import jax.numpy as jnp
from jax import lax

D = 2048
FF = 8192
HQ = 32
HK = 8
HEAD = 64
CONT = 4
GTOK = 512
GROUPS = 8


def draw_seq_lengths(key, part):
    key = jax.random.fold_in(key, 11)
    chosen_key, rest = jax.random.split(key)
    chosen = jax.random.randint(chosen_key, (), 0, GROUPS)
    keys = jax.random.split(rest, GROUPS)

    def single(sub, index):
        first, second = jax.random.split(sub)
        extra = jax.random.randint(first, (), 0, GTOK // 4 + 1)
        extra = jnp.where(index == chosen, GTOK // 4, extra)
        prompt = GTOK // 2 + extra
        remain = GTOK - prompt
        weights = jax.random.randint(second, (CONT,), 1, 5)
        shares = jnp.maximum(1, remain * weights // jnp.sum(weights))
        shares = shares.at[CONT - 1].set(remain - jnp.sum(shares[:CONT - 1]))
        return jnp.concatenate([prompt[None], shares]).astype(jnp.int32)
    return jax.vmap(single)(keys, jnp.arange(GROUPS)).astype(jnp.int32)


def block_levels(own_key, shape, cuts, smallest, high):
    factor_of, own = 1.0, jax.random.fold_in(own_key, 6)
    for position, shards_of in cuts:
        draws = jnp.exp(jax.random.uniform(jax.random.fold_in(own, position), (shards_of,), jnp.float32, smallest / len(cuts), high / len(cuts)))
        factor_of = factor_of * jnp.repeat(draws, shape[position] // shards_of).reshape([-1 if axis == position else 1 for axis in range(len(shape))])
    return factor_of


def bell_draw(stream_key, dims, deviation, reach, cuts=(), kind=jnp.bfloat16):
    loudness = block_levels(stream_key, dims, cuts, -0.22, 0.18) if cuts else 1.0
    array = jax.random.normal(stream_key, dims, jnp.float32) * deviation * loudness
    return jnp.minimum(jnp.maximum(array, -reach), reach).astype(kind)


def setup_inputs(seed: int = 0) -> dict:
    streams_of = jax.random.split(jax.random.key(seed), 13)
    tokens = bell_draw(streams_of[0], (GROUPS, GTOK, D), 1.0, 6.0, ((0, 8), (1, 4)))
    seq_lengths = draw_seq_lengths(jax.random.fold_in(streams_of[12], 71), 0)
    attn_gain = jnp.clip(1.0 + 0.1 * jax.random.normal(streams_of[2], (D,), jnp.float32), 0.5, 1.5).astype(jnp.bfloat16)
    w_query = bell_draw(streams_of[3], (D, HQ * HEAD), D ** -0.5, 0.125, ((0, 4),))
    w_key = bell_draw(streams_of[4], (D, HK * HEAD), D ** -0.5, 0.125, ((0, 4),))
    w_value = bell_draw(streams_of[5], (D, HK * HEAD), D ** -0.5, 0.125, ((0, 4),))
    w_out = bell_draw(streams_of[6], (HQ * HEAD, D), (HQ * HEAD // 16) ** -0.5, 0.5, ((0, 4),))
    mlp_gain = jnp.clip(1.0 + 0.1 * jax.random.normal(streams_of[7], (D,), jnp.float32), 0.5, 1.5).astype(jnp.bfloat16)
    w_gate = bell_draw(streams_of[8], (D, FF), D ** -0.5, 0.125, ((0, 4),))
    w_up = bell_draw(streams_of[9], (D, FF), D ** -0.5, 0.125, ((0, 4),))
    w_down = bell_draw(streams_of[10], (FF, D), (FF // 4) ** -0.5, 0.125, ((0, 4),))
    cotangent = bell_draw(streams_of[11], (GROUPS, GTOK, D), 1.0, 6.0, ((0, 8), (1, 4)))
    return dict(tokens=tokens, seq_lengths=seq_lengths, attn_gain=attn_gain, w_query=w_query, w_key=w_key, w_value=w_value, w_out=w_out, mlp_gain=mlp_gain, w_gate=w_gate, w_up=w_up, w_down=w_down, cotangent=cotangent)


EPS = 1e-05
BASE = 500000.0
MASKED = -1e+30

@jax.custom_vjp
def low(v):
    return lax.optimization_barrier(v.astype(jnp.bfloat16)).astype(jnp.float32)

@jax.custom_vjp
def low_back(v):
    return v

def low_keep(v):
    return (low(v), None)

def low_pass(kept, grad):
    return (grad,)

def back_keep(v):
    return (v, None)

def back_low(kept, grad):
    return (low(grad),)
low.defvjp(low_keep, low_pass)
low_back.defvjp(back_keep, back_low)

def dense(left, right):
    return jnp.dot(left, right, precision=lax.Precision.HIGHEST)

def positions_of(lengths, total):
    lengths = lengths.astype(jnp.int32)
    ends = jnp.cumsum(lengths).astype(jnp.int32)
    starts = (ends - lengths).astype(jnp.int32)
    index = jnp.arange(total, dtype=jnp.int32)
    segment = lax.optimization_barrier(jnp.sum((index[:, None] >= ends[None, :-1]).astype(jnp.int32), axis=1)).astype(jnp.int32)
    member = segment[:, None] == jnp.arange(lengths.shape[0], dtype=jnp.int32)[None, :]
    start = lax.optimization_barrier(jnp.sum(jnp.where(member, starts[None, :], 0), axis=1)).astype(jnp.int32)
    place = jnp.where(segment == 0, index, lengths[0] + index - start).astype(jnp.int32)
    return (segment, place)

def allowed_of(seg_query, place_query, seg_key, place_key):
    same = (seg_key[None, :] == 0) | (seg_key[None, :] == seg_query[:, None])
    return same & (place_key[None, :] <= place_query[:, None])

def rope_tables(place, size):
    half = size // 2
    freq = BASE ** (-(2.0 * jnp.arange(half, dtype=jnp.float32)) / size)
    angle = place.astype(jnp.float32)[:, None] * freq[None, :]
    return (jnp.cos(angle)[:, None, :], jnp.sin(angle)[:, None, :])

def rotate(value, cosine, sine):
    half = value.shape[-1] // 2
    first, second = (value[..., :half], value[..., half:])
    return jnp.concatenate([first * cosine - second * sine, second * cosine + first * sine], axis=-1)

def rms_norm(value, gain):
    return value * lax.rsqrt(lax.optimization_barrier(jnp.mean(value * value, axis=-1, keepdims=True)) + EPS) * gain

def attend_block(q_block, seg_block, place_block, keys, values, segment, place):
    scale = HEAD ** (-0.5)
    scores = jnp.einsum('bhgd,khd->hgbk', q_block, keys, precision=lax.Precision.HIGHEST) * scale
    scores = low_back(scores)
    allowed = allowed_of(seg_block, place_block, segment, place)
    scores = jnp.where(allowed[None, None], scores, MASKED)
    top = lax.optimization_barrier(jnp.max(scores, axis=-1, keepdims=True))
    expo = jnp.exp(scores - top)
    probs = low(expo / lax.optimization_barrier(jnp.sum(expo, axis=-1, keepdims=True)))
    out = jnp.einsum('hgbk,khd->bhgd', probs, values, precision=lax.Precision.HIGHEST)
    return out.reshape(q_block.shape[0], HQ * HEAD)

def attend(query, keys, values, segment, place):
    total = query.shape[0]
    block = min(512, total)
    count = total // block
    groups = HQ // HK
    q_blocks = query.reshape(count, block, HK, groups, HEAD)
    seg_blocks = segment.reshape(count, block)
    place_blocks = place.reshape(count, block)
    checked = jax.checkpoint(attend_block)

    def one(args):
        return checked(args[0], args[1], args[2], keys, values, segment, place)
    out = lax.map(one, (q_blocks, seg_blocks, place_blocks))
    return out.reshape(total, HQ * HEAD)

def group_layer(params, x, lengths):
    attn_gain, w_query, w_key, w_value, w_out, mlp_gain, w_gate, w_up, w_down = params
    total = x.shape[0]
    segment, place = positions_of(lengths, total)
    cosine, sine = rope_tables(place, HEAD)
    normed_one = low(rms_norm(x, attn_gain))
    query_pre = low_back(dense(normed_one, w_query))
    key_pre = low_back(dense(normed_one, w_key))
    value = low(low_back(dense(normed_one, w_value))).reshape(total, HK, HEAD)
    query = low(rotate(query_pre.reshape(total, HQ, HEAD), cosine, sine))
    keys = low(rotate(key_pre.reshape(total, HK, HEAD), cosine, sine))
    attended = low(low_back(attend(query, keys, value, segment, place)))
    mid = x + low_back(dense(attended, w_out))
    normed_two = low(rms_norm(mid, mlp_gain))
    gate = low_back(dense(normed_two, w_gate))
    up = low_back(dense(normed_two, w_up))
    active = low(jax.nn.sigmoid(gate) * gate * up)
    return mid + low_back(dense(active, w_down))

def reference(tokens, seq_lengths, attn_gain, w_query, w_key, w_value, w_out, mlp_gain, w_gate, w_up, w_down, cotangent):
    params = tuple((a.astype(jnp.float32) for a in (attn_gain, w_query, w_key, w_value, w_out, mlp_gain, w_gate, w_up, w_down)))
    inputs = tokens.astype(jnp.float32)
    checked = jax.checkpoint(group_layer)

    def forward(x_all, weights):
        return lax.map(lambda args: checked(weights, args[0], args[1]), (x_all, seq_lengths))
    result, pull = jax.vjp(forward, inputs, params)
    grad_inputs, grads = pull(cotangent.astype(jnp.float32))
    return (result.astype(jnp.bfloat16), grad_inputs.astype(jnp.bfloat16), grads[0], grads[1], grads[2], grads[3], grads[4], grads[5], grads[6], grads[7], grads[8])
```

```python
import jax
import jax.numpy as jnp
from jax import lax
from jax.sharding import Mesh
from jax.sharding import PartitionSpec as P

HQ = 32
HK = 8
HEAD = 64

EPS = 1e-05
BASE = 500000.0
MASKED = -1e30

BF = jnp.bfloat16
F32 = jnp.float32


def positions_of(lengths, index):
    ends = jnp.cumsum(lengths)
    starts = ends - lengths
    segment = jnp.sum((index[:, None] >= ends[None, :-1]).astype(jnp.int32), axis=1)
    member = segment[:, None] == jnp.arange(lengths.shape[0], dtype=jnp.int32)[None, :]
    start = jnp.sum(jnp.where(member, starts[None, :], 0), axis=1)
    place = jnp.where(segment == 0, index, lengths[0] + index - start)
    return (segment, place)


def allowed_of(segment, place):
    same = (segment[None, :] == 0) | (segment[None, :] == segment[:, None])
    return same & (place[None, :] <= place[:, None])


def rope_tables(place, size):
    half = size // 2
    freq = BASE ** (-(2.0 * jnp.arange(half, dtype=F32)) / size)
    angle = place.astype(F32)[:, None] * freq[None, :]
    return (jnp.cos(angle)[:, None, :], jnp.sin(angle)[:, None, :])


def rotate(value, cosine, sine):
    half = value.shape[-1] // 2
    first, second = (value[..., :half], value[..., half:])
    return jnp.concatenate(
        [first * cosine - second * sine, second * cosine + first * sine], axis=-1
    )


def rotate_back(grad, cosine, sine):
    half = grad.shape[-1] // 2
    first, second = (grad[..., :half], grad[..., half:])
    return jnp.concatenate(
        [first * cosine + second * sine, second * cosine - first * sine], axis=-1
    )


def matmul(left, right):
    return jnp.dot(left, right, preferred_element_type=F32)


def contract_last(left, right):
    return lax.dot_general(left, right, (((1,), (1,)), ((), ())), preferred_element_type=F32)


def contract_first(left, right):
    return lax.dot_general(left, right, (((0,), (0,)), ((), ())), preferred_element_type=F32)


def norm_back(grad_normed, unit, inverse, gain):
    scaled = grad_normed * gain
    return inverse * (scaled - unit * jnp.mean(scaled * unit, axis=1, keepdims=True))


def step_to(value, axis, step):
    size = lax.axis_size(axis)
    return lax.ppermute(value, axis, [(i, i ^ step) for i in range(size)])


def fetch(blocks):
    return [blocks[0]] + [step_to(b, "group", s) for s, b in enumerate(blocks) if s]


def gather_plane(mine):
    parts = lax.axis_size("group")
    got = fetch([mine] * parts)
    if lax.axis_size("core") == 1:
        return jnp.concatenate(got, axis=0)
    return jnp.concatenate(got + [step_to(g, "core", 1) for g in got], axis=0)


def scatter_plane(partial):
    parts = lax.axis_size("group")
    if lax.axis_size("core") == 2:
        half = partial.shape[0] // 2
        other = step_to(partial[half:].astype(BF), "core", 1)
        partial = partial[:half] + other.astype(F32)
    rows = partial.shape[0] // parts
    blocks = [partial[:rows]] + [
        partial[s * rows : (s + 1) * rows].astype(BF) for s in range(1, parts)
    ]
    got = fetch(blocks)
    total = got[0]
    for other in got[1:]:
        total = total + other.astype(F32)
    return total


def sum_rest(value):
    size = lax.axis_size("rest")
    if size != 4:
        return lax.psum(value, "rest")
    place = lax.axis_index("rest")
    inner = (place == 1) | (place == 2)
    value = value + lax.ppermute(value, "rest", [(0, 1), (3, 2)])
    value = value + lax.ppermute(value, "rest", [(1, 2), (2, 1)])
    outer = lax.ppermute(value, "rest", [(1, 0), (2, 3)])
    return jnp.where(inner, value, outer)


def both_cores(value):
    if lax.axis_size("core") == 1:
        return value[None]
    other = step_to(value, "core", 1)
    core = lax.axis_index("core")
    return jnp.stack([jnp.where(core == 0, value, other), jnp.where(core == 0, other, value)])


def body(
    tokens,
    seq_lengths,
    attn_gain,
    w_query,
    w_key,
    w_value,
    w_out,
    mlp_gain,
    w_gate,
    w_up,
    w_down,
    cotangent,
):
    parts = lax.axis_size("group")
    cores = lax.axis_size("core")
    g = lax.axis_index("group")
    c = lax.axis_index("core")
    rows, width = tokens.shape[1:]
    total = rows * parts
    team = parts * cores
    heads = HQ // HK
    scale = HEAD ** (-0.5)
    ff = w_gate.shape[1] // team
    share = w_gate.shape[0]
    qw = HQ * HEAD // team
    kw = HK * HEAD // team
    assert kw == HEAD

    def member(s):
        return (g ^ s) * cores + c

    def columns(weight, size, s):
        return lax.dynamic_slice_in_dim(weight, member(s) * size, size, 1)

    def in_order(got):
        out = jnp.zeros((parts,) + got[0].shape, got[0].dtype)
        for s, block in enumerate(got):
            out = lax.dynamic_update_slice_in_dim(out, block[None], g ^ s, 0)
        return out.reshape((parts * got[0].shape[0],) + got[0].shape[1:])

    x_mine = tokens[0]
    x_all = gather_plane(x_mine)
    gains = in_order(fetch([jnp.stack([attn_gain, mlp_gain], axis=1)] * parts))
    gain_one = gains[:, 0].astype(F32)
    gain_two = gains[:, 1].astype(F32)
    qkv_full = in_order(
        fetch(
            [
                jnp.concatenate(
                    [columns(w_query, qw, s), columns(w_key, kw, s), columns(w_value, kw, s)],
                    axis=1,
                )
                for s in range(parts)
            ]
        )
    )
    gate_full = in_order(fetch([columns(w_gate, ff, s) for s in range(parts)]))
    up_full = in_order(fetch([columns(w_up, ff, s) for s in range(parts)]))
    out_rows = lax.dynamic_slice_in_dim(w_out, c * qw, qw, 0)
    down_rows = lax.dynamic_slice_in_dim(w_down, c * ff, ff, 0)
    cot_all = gather_plane(cotangent[0])

    lengths = [seq_lengths[0]]
    if cores == 2:
        lengths.append(step_to(seq_lengths[0], "core", 1))
    index = jnp.concatenate(
        [(g ^ s) * rows + jnp.arange(rows, dtype=jnp.int32) for s in range(parts)]
    )
    marks = [positions_of(one, index) for one in lengths]
    allowed = [jnp.tile(allowed_of(*m), (heads, 1)) for m in marks]
    tables = [rope_tables(m[1], HEAD) for m in marks]

    x = x_all.astype(F32)
    inverse_all = lax.rsqrt(jnp.mean(x * x, axis=1, keepdims=True) + EPS)
    normed_one = (x * inverse_all * gain_one).astype(BF)
    qkv = matmul(normed_one, qkv_full)

    def stack_heads(value):
        return value.reshape(total, heads, HEAD).transpose(1, 0, 2).reshape(heads * total, HEAD)

    def lay_heads(value):
        return value.reshape(heads, total, HEAD).transpose(1, 0, 2).reshape(total, heads * HEAD)

    kept = []
    attended = []
    for j in range(cores):
        one = qkv[j * total : (j + 1) * total]
        query = rotate(one[:, :qw].reshape(total, heads, HEAD), *tables[j]).astype(BF)
        query = stack_heads(query.reshape(total, qw))
        key = rotate(one[:, qw : qw + kw].reshape(total, 1, HEAD), *tables[j]).astype(BF)[:, 0]
        value = one[:, qw + kw :].astype(BF)
        scores = jnp.where(allowed[j], contract_last(query, key) * scale, MASKED)
        top = jnp.max(scores, axis=1, keepdims=True)
        expo = jnp.exp(scores - top)
        probs = expo / jnp.sum(expo, axis=1, keepdims=True)
        attended.append(lay_heads(matmul(probs.astype(BF), value)).astype(BF))
        kept.append((query, key, value, probs))
    attended = jnp.concatenate(attended, axis=0)

    x_own = x_mine.astype(F32)
    mid = x_own + scatter_plane(matmul(attended, out_rows))
    inverse_two = lax.rsqrt(jnp.mean(mid * mid, axis=1, keepdims=True) + EPS)
    unit_two = mid * inverse_two
    normed_two = gather_plane((unit_two * gain_two).astype(BF))

    gate = matmul(normed_two, gate_full)
    up = matmul(normed_two, up_full)
    sigma = jax.nn.sigmoid(gate)
    active = (gate * sigma * up).astype(BF)
    grad_active = contract_last(cot_all, down_rows)
    grad_gate_pre = (grad_active * up * sigma * (1.0 + gate * (1.0 - sigma))).astype(BF)
    grad_up_pre = (grad_active * gate * sigma).astype(BF)
    grad_normed_two = scatter_plane(
        contract_last(grad_gate_pre, gate_full) + contract_last(grad_up_pre, up_full)
    )
    grad_down = contract_first(active, cot_all).astype(BF)
    grad_gate = contract_first(normed_two, grad_gate_pre).astype(BF)
    grad_up = contract_first(normed_two, grad_up_pre).astype(BF)
    result = mid + scatter_plane(matmul(active, down_rows))

    def turn(grad):
        return fetch(
            [lax.dynamic_slice_in_dim(grad, (g ^ s) * share, share, 0) for s in range(parts)]
        )

    def finish_columns(blocks, size):
        out = jnp.zeros((share, parts, cores, size), F32)
        for s, block in enumerate(blocks):
            pair = both_cores(sum_rest(block)).astype(F32).transpose(1, 0, 2)
            out = lax.dynamic_update_slice_in_dim(out, pair[:, None], g ^ s, 1)
        return out.reshape(share, parts * cores * size)

    def finish_rows(grad, pieces):
        size = grad.shape[0] // pieces
        got = [
            both_cores(sum_rest(grad[i * size : (i + 1) * size])).astype(F32)
            for i in range(pieces)
        ]
        return jnp.stack(got, axis=1).reshape(cores * grad.shape[0], grad.shape[1])

    grad_y = cotangent[0].astype(F32)
    grad_gain_two = jnp.sum(grad_normed_two * unit_two, axis=0)
    grad_mid = grad_y + norm_back(grad_normed_two, unit_two, inverse_two, gain_two)
    grad_branch = gather_plane(grad_mid.astype(BF))
    grad_attended = contract_last(grad_branch, out_rows).astype(BF)
    grad_out = contract_first(attended, grad_branch).astype(BF)

    grad_qkv = []
    for j in range(cores):
        query, key, value, probs = kept[j]
        g_head = stack_heads(grad_attended[j * total : (j + 1) * total])
        grad_p = contract_last(g_head, value)
        grad_s = (probs * (grad_p - jnp.sum(probs * grad_p, axis=1, keepdims=True))).astype(BF)
        grad_q = lay_heads(matmul(grad_s, key) * scale).reshape(total, heads, HEAD)
        grad_k = (contract_first(grad_s, query) * scale)[:, None]
        grad_v = contract_first(probs.astype(BF), g_head)
        grad_qkv.append(
            jnp.concatenate(
                [
                    rotate_back(grad_q, *tables[j]).reshape(total, qw),
                    rotate_back(grad_k, *tables[j]).reshape(total, kw),
                    grad_v,
                ],
                axis=1,
            ).astype(BF)
        )
    grad_qkv = jnp.concatenate(grad_qkv, axis=0)
    grad_normed_one = scatter_plane(contract_last(grad_qkv, qkv_full))
    inverse_one = inverse_all[:rows]
    unit_one = x_own * inverse_one
    grad_gain_one = jnp.sum(grad_normed_one * unit_one, axis=0)
    grad_x = grad_mid + norm_back(grad_normed_one, unit_one, inverse_one, gain_one)
    grad_weights = contract_first(normed_one, grad_qkv).astype(BF)

    grad_gains = lax.psum(
        jnp.stack([grad_gain_one, grad_gain_two]), ("group", "rest", "core")
    )
    grad_gains = lax.dynamic_slice_in_dim(grad_gains, g * share, share, 1)

    turned = turn(grad_weights)
    grad_qkv_rows = finish_columns(turned, qw + 2 * kw).reshape(share, team, qw + 2 * kw)
    return (
        result.astype(BF)[None],
        grad_x.astype(BF)[None],
        grad_gains[0],
        grad_qkv_rows[:, :, :qw].reshape(share, team * qw),
        grad_qkv_rows[:, :, qw : qw + kw].reshape(share, team * kw),
        grad_qkv_rows[:, :, qw + kw :].reshape(share, team * kw),
        finish_rows(grad_out, 1),
        grad_gains[1],
        finish_columns(turn(grad_gate), ff),
        finish_columns(turn(grad_up), ff),
        finish_rows(grad_down, 4),
    )


def solution(mesh):
    parts, replicas = mesh.devices.shape
    cores = 2 if HK % (2 * parts) == 0 and replicas % 2 == 0 else 1
    split = Mesh(
        mesh.devices.reshape(parts, replicas // cores, cores), ("group", "rest", "core")
    )
    replica = ("rest", "core")
    weights = (P("group"),) + (P("group", None),) * 4 + (P("group"),) + (P("group", None),) * 3
    split_tokens = P(replica, "group", None)
    return jax.shard_map(
        body,
        mesh=split,
        in_specs=(split_tokens, P(replica, None)) + weights + (split_tokens,),
        out_specs=(split_tokens, split_tokens) + weights,
        check_vma=False,
    )
```

```python
import jax
import jax.numpy as jnp
from jax import lax
from jax.experimental import pallas as pl
from jax.experimental.pallas import tpu as pltpu
from jax.sharding import Mesh
from jax.sharding import PartitionSpec as P

HQ = 32
HK = 8
HEAD = 64

EPS = 1e-05
BASE = 500000.0
MASKED = -1e30

BF = jnp.bfloat16
F32 = jnp.float32


def positions_of(lengths, index):
    ends = jnp.cumsum(lengths)
    starts = ends - lengths
    segment = jnp.sum((index[:, None] >= ends[None, :-1]).astype(jnp.int32), axis=1)
    member = segment[:, None] == jnp.arange(lengths.shape[0], dtype=jnp.int32)[None, :]
    start = jnp.sum(jnp.where(member, starts[None, :], 0), axis=1)
    place = jnp.where(segment == 0, index, lengths[0] + index - start)
    return (segment, place)


def matmul(left, right):
    return jnp.dot(left, right, preferred_element_type=F32)


def contract_last(left, right):
    return lax.dot_general(left, right, (((1,), (1,)), ((), ())), preferred_element_type=F32)


def contract_first(left, right):
    return lax.dot_general(left, right, (((0,), (0,)), ((), ())), preferred_element_type=F32)


def norm_back(grad_normed, unit, inverse, gain):
    scaled = grad_normed * gain
    return inverse * (scaled - unit * jnp.mean(scaled * unit, axis=1, keepdims=True))


def after(value, *others):
    return lax.optimization_barrier((value,) + others)[0]


def after(value, *others):
    return lax.optimization_barrier((value,) + others)[0]


def step_to(value, axis, step):
    size = lax.axis_size(axis)
    return lax.ppermute(value, axis, [(i, i ^ step) for i in range(size)])


def exchange(blocks):
    return lax.all_to_all(blocks, "group", 0, 0, tiled=True)


def spread(mine):
    parts = lax.axis_size("group")
    blocks = exchange(jnp.broadcast_to(mine[None], (parts,) + mine.shape))
    return blocks.reshape((parts * mine.shape[0],) + mine.shape[1:])


def from_core(value):
    return step_to(value, "core", 1)


def with_core(got):
    if lax.axis_size("core") == 1:
        return got
    return jnp.concatenate([got, from_core(got)], axis=0)


def scatter_send(partial):
    parts = lax.axis_size("group")
    if lax.axis_size("core") == 2:
        half = partial.shape[0] // 2
        partial = partial[:half] + from_core(partial[half:].astype(BF)).astype(F32)
    rows = partial.shape[0] // parts
    return partial.astype(BF).reshape((parts, rows) + partial.shape[1:])


def scatter_sum(blocks):
    return jnp.sum(exchange(blocks).astype(F32), axis=0)


def rotated(value, cosine, sine, back):
    wide = value.shape[1]
    half = HEAD // 2
    lane = lax.broadcasted_iota(jnp.int32, value.shape, 1)
    low = lane % HEAD < half
    other = jnp.where(
        low, pltpu.roll(value, wide - half, 1), pltpu.roll(value, half, 1)
    )
    sign = jnp.where(low, -1.0, 1.0)
    if back:
        sign = -sign
    return value * cosine + other * sign * sine


def visible(place_query, segment_query, place_key, segment_key):
    same = (segment_key == 0) | (segment_key == segment_query)
    return same & (place_key <= place_query)


def forward_kernel(qkv_ref, cos_ref, sin_ref, column_ref, row_ref, o_ref, kept_ref, lse_ref):
    heads = HQ // HK
    wide = heads * HEAD
    scale = HEAD ** (-0.5)
    cosine, sine = cos_ref[...], sin_ref[...]
    tiles = wide // cosine.shape[1]
    query = rotated(
        qkv_ref[:, :wide],
        jnp.concatenate([cosine] * tiles, axis=1),
        jnp.concatenate([sine] * tiles, axis=1),
        False,
    )
    query = query.astype(BF)
    pair = qkv_ref[:, wide:]
    lane = lax.broadcasted_iota(jnp.int32, pair.shape, 1)
    pair = jnp.where(lane < HEAD, rotated(pair, cosine, sine, False), pair).astype(BF)
    kept_ref[:, :wide] = query
    kept_ref[:, wide:] = pair
    key, value = pair[:, :HEAD], pair[:, HEAD:]
    allowed = visible(column_ref[:, 0:1], column_ref[:, 1:2], row_ref[0:1, :], row_ref[1:2, :])
    found = []
    for h in range(heads):
        one = query[:, h * HEAD : (h + 1) * HEAD]
        scores = jnp.where(allowed, contract_last(one, key) * scale, MASKED)
        top = jnp.max(scores, axis=1, keepdims=True)
        expo = jnp.exp(scores - top)
        denom = jnp.sum(expo, axis=1, keepdims=True)
        probs = (expo / denom).astype(BF)
        o_ref[:, h * HEAD : (h + 1) * HEAD] = matmul(probs, value).astype(BF)
        found.append(top + jnp.log(denom))
    place = lax.broadcasted_iota(jnp.int32, lse_ref.shape, 1)
    total = jnp.zeros(lse_ref.shape, F32)
    for h in range(heads):
        total = jnp.where(place == h, found[h], total)
    lse_ref[...] = total


def backward_kernel(
    kept_ref, lse_ref, grad_ref, cos_ref, sin_ref, column_ref, row_ref, out_ref, hold_ref
):
    heads = HQ // HK
    wide = heads * HEAD
    scale = HEAD ** (-0.5)
    key = kept_ref[:, wide : wide + HEAD]
    value = kept_ref[:, wide + HEAD :]
    allowed = visible(column_ref[:, 0:1], column_ref[:, 1:2], row_ref[0:1, :], row_ref[1:2, :])
    total = key.shape[0]
    grad_k = jnp.zeros((total, HEAD), F32)
    grad_v = jnp.zeros((total, HEAD), F32)
    for h in range(heads):
        one = kept_ref[:, h * HEAD : (h + 1) * HEAD]
        grad = grad_ref[:, h * HEAD : (h + 1) * HEAD]
        scores = jnp.where(allowed, contract_last(one, key) * scale, MASKED)
        probs = jnp.exp(scores - lse_ref[:, h : h + 1])
        grad_p = contract_last(grad, value)
        grad_s = probs * (grad_p - jnp.sum(probs * grad_p, axis=1, keepdims=True))
        grad_s = grad_s.astype(BF)
        hold_ref[:, h * HEAD : (h + 1) * HEAD] = matmul(grad_s, key) * scale
        grad_k = grad_k + contract_first(grad_s, one)
        grad_v = grad_v + contract_first(probs.astype(BF), grad)
    hold_ref[:, wide : wide + HEAD] = grad_k * scale
    hold_ref[:, wide + HEAD :] = grad_v
    cosine, sine = cos_ref[...], sin_ref[...]
    tiles = wide // cosine.shape[1]
    out_ref[:, :wide] = rotated(
        hold_ref[:, :wide],
        jnp.concatenate([cosine] * tiles, axis=1),
        jnp.concatenate([sine] * tiles, axis=1),
        True,
    ).astype(BF)
    pair = hold_ref[:, wide:]
    lane = lax.broadcasted_iota(jnp.int32, pair.shape, 1)
    pair = jnp.where(lane < HEAD, rotated(pair, cosine, sine, True), pair)
    out_ref[:, wide:] = pair.astype(BF)


def by_group(kernel, total, groups, inputs, outputs, scratch=()):
    def spec(shape):
        if len(shape) == 3:
            return pl.BlockSpec((None,) + shape[1:], lambda i: (i, 0, 0))
        return pl.BlockSpec((total, shape[1]), lambda i: (i, 0))

    return pl.pallas_call(
        kernel,
        grid=(groups,),
        in_specs=[spec(one.shape) for one in inputs],
        out_specs=[spec(one.shape) for one in outputs],
        out_shape=list(outputs),
        scratch_shapes=list(scratch),
        compiler_params=pltpu.CompilerParams(vmem_limit_bytes=40 * 2**20),
        cost_estimate=pl.CostEstimate(flops=0, bytes_accessed=1, transcendentals=0),
    )(*inputs)


class Clock:
    def __init__(self):
        self.token = jnp.zeros((8, 128), F32)

    def tick(self, *values):
        flat, tree = jax.tree.flatten(values)
        out = lax.optimization_barrier((self.token, *flat))
        self.token = out[0]
        values = jax.tree.unflatten(tree, out[1:])
        return values[0] if len(values) == 1 else values

    def now(self, value):
        return after(value, self.token)


class Line:
    def __init__(self, clock, shape):
        self.clock = clock
        self.shape = shape
        place = lax.axis_index("rest")
        self.inner = (place == 1) | (place == 2)
        self.sums = {}
        self.flight = {}

    def piece(self, array, block):
        rows, wide = self.shape
        if array.ndim == 3:
            return array[block[0]]
        row, column = block
        return array[row * rows : (row + 1) * rows, column * wide : (column + 1) * wide]

    def slot(self, entering, *values):
        last = self.flight
        came, moved, values = self.clock.tick(last.get("came"), last.get("moved"), values)
        flight = {}
        send = None
        if last.get("across"):
            name, part = last["across"]
            full = (part.astype(F32) + moved.astype(F32)).astype(BF)
            flight["out"] = (name, full)
            send = full
        if entering is not None:
            name, array, block = entering
            array = self.clock.now(array)
            flight["enter"] = (name, array, block)
            piece = self.piece(array, block)
            send = piece if send is None else jnp.where(self.inner, send, piece)
        if last.get("enter"):
            name, array, block = last["enter"]
            part = (self.piece(array, block).astype(F32) + came.astype(F32)).astype(BF)
            flight["across"] = (name, part)
            flight["moved"] = lax.ppermute(part, "rest", [(1, 2), (2, 1)])
        if send is not None:
            flight["came"] = lax.ppermute(send, "rest", [(0, 1), (1, 0), (2, 3), (3, 2)])
        if last.get("out"):
            name, full = last["out"]
            self.sums[name] = jnp.where(self.inner, full, came)
        self.flight = flight
        return values[0] if len(values) == 1 else values

    def stack(self, name, count):
        return jnp.stack([self.sums[name, k] for k in range(count)])


def place(shape, mine, other, rows, wide, blocks):
    core = lax.axis_index("core")
    table = jnp.asarray(
        [[list(there) + list(here(k)) for k in range(2)] for there, here in blocks], jnp.int32
    )
    table = jnp.stack([table[:, 0], table[:, 1]])
    table = jnp.where(core == 0, table, table[::-1])
    count = len(blocks)
    table = table.reshape(-1)
    size = table.shape[0] // (2 * count)

    def entry(w, k, j, field):
        return w[(k * count + j) * size + field]

    def source(k, j, w, own):
        j = jnp.where(k == own, j, count - 1 if own == 0 else 0)
        return tuple(entry(w, k, j, field) for field in range(3))

    def kernel(table_ref, mine_ref, other_ref, out_ref):
        @pl.when(pl.program_id(0) == 0)
        def _():
            out_ref[...] = mine_ref[...].astype(F32)

        @pl.when(pl.program_id(0) == 1)
        def _():
            out_ref[...] = other_ref[...].astype(F32)

    return pl.pallas_call(
        kernel,
        grid_spec=pltpu.PrefetchScalarGridSpec(
            num_scalar_prefetch=1,
            grid=(2, count),
            in_specs=[
                pl.BlockSpec((None, rows, wide), lambda k, j, w: source(k, j, w, 0)),
                pl.BlockSpec((None, rows, wide), lambda k, j, w: source(k, j, w, 1)),
            ],
            out_specs=pl.BlockSpec(
                (rows, wide), lambda k, j, w: (entry(w, k, j, 3), entry(w, k, j, 4))
            ),
        ),
        out_shape=jax.ShapeDtypeStruct(shape, F32),
        compiler_params=pltpu.CompilerParams(vmem_limit_bytes=16 * 2**20),
        cost_estimate=pl.CostEstimate(
            flops=0, bytes_accessed=12 * count * rows * wide, transcendentals=0
        ),
    )(table, mine, other)


def body(
    tokens,
    seq_lengths,
    attn_gain,
    w_query,
    w_key,
    w_value,
    w_out,
    mlp_gain,
    w_gate,
    w_up,
    w_down,
    cotangent,
):
    parts = lax.axis_size("group")
    cores = lax.axis_size("core")
    g = lax.axis_index("group")
    c = lax.axis_index("core")
    rows, width = tokens.shape[1:]
    total = rows * parts
    team = parts * cores
    heads = HQ // HK
    scale = HEAD ** (-0.5)
    ff = w_gate.shape[1] // team
    share = w_gate.shape[0]
    qw = HQ * HEAD // team
    kw = HK * HEAD // team
    assert kw == HEAD

    def columns(weight, size, rows=slice(None)):
        return jnp.stack(
            [
                lax.dynamic_slice_in_dim(weight[rows], (k * cores + c) * size, size, 1)
                for k in range(parts)
            ]
        )

    def fetch(blocks):
        return [
            step_to(lax.dynamic_index_in_dim(blocks, g ^ s, 0, keepdims=False), "group", s)
            for s in range(1, parts)
        ]

    def in_order(own, got):
        out = jnp.zeros((parts,) + own.shape, own.dtype)
        for s, block in enumerate([own] + got):
            out = lax.dynamic_update_slice_in_dim(out, block[None], g ^ s, 0)
        return out.reshape((parts * own.shape[0],) + own.shape[1:])

    def own_columns(weight, size):
        return lax.dynamic_slice_in_dim(weight, (g * cores + c) * size, size, 1)

    clock = Clock()
    x_mine = tokens[0]
    extra = 2 * share // width if 2 * share > width else 1
    gains = jnp.concatenate([attn_gain, mlp_gain])
    gains = jnp.pad(gains, (0, 16 * width - gains.shape[0])).reshape(16, width)
    x_got = spread(jnp.concatenate([x_mine, gains], axis=0))
    x_got = x_got.reshape(parts, rows + 16, width)
    gains = x_got[:, rows].reshape(parts, width)[:, : 2 * share]
    gain_one = gains[:, :share].reshape(-1).astype(F32)
    gain_two = gains[:, share:].reshape(-1).astype(F32)
    x_got = x_got[:, :rows].reshape(parts * rows, width)
    qkv_send = jnp.concatenate(
        [columns(w_query, qw), columns(w_key, kw), columns(w_value, kw)], axis=2
    )
    qkv_got = fetch(qkv_send)
    qkv_own = lax.dynamic_index_in_dim(qkv_send, g, 0, keepdims=False)

    paired = lax.axis_size("rest") == 4
    even = lax.axis_index("rest") % 2 == 0
    halves = [slice(0, share // 4 * 3), slice(share // 4 * 3, share)]
    sends = []
    for half in halves:
        gate_send = columns(w_gate, ff, half)
        up_send = columns(w_up, ff, half)
        sends.append([jnp.where(even, gate_send, up_send)] if paired else [gate_send, up_send])
    lengths = [seq_lengths[0]]
    if cores == 2:
        lengths.append(from_core(seq_lengths[0]))
    index = jnp.arange(total, dtype=jnp.int32)
    marks = [positions_of(one, index) for one in lengths]
    half = HEAD // 2
    freq = BASE ** (-(2.0 * jnp.arange(half, dtype=F32)) / HEAD)
    place_all = jnp.concatenate([one[1] for one in marks]).astype(F32)
    angle = place_all[:, None] * jnp.tile(freq, 128 // half)[None, :]
    cosine, sine = jnp.cos(angle), jnp.sin(angle)
    marks_row = jnp.stack([jnp.stack([one[1], one[0]]) for one in marks])
    marks_column = marks_row.transpose(0, 2, 1)
    x_got, qkv_got, sends, cosine, sine, marks_row, marks_column = clock.tick(
        x_got, qkv_got, sends, cosine, sine, marks_row, marks_column
    )

    out_rows = lax.dynamic_slice_in_dim(w_out, c * qw, qw, 0)
    down_rows = lax.dynamic_slice_in_dim(w_down, c * ff, ff, 0)
    first_got = [[fetch(one) for one in sends[0]]]
    second_got = []
    qkv_full = in_order(qkv_own, qkv_got)
    x_all = with_core(x_got)

    def swap(got):
        return step_to(jnp.stack(got[0]), "rest", 1)

    def fill(out, got, row):
        for s in range(1, parts):
            out = lax.dynamic_update_slice(out, got[s - 1][None], (g ^ s, row, 0))
        return out

    def begin(own):
        return lax.dynamic_update_slice_in_dim(
            jnp.zeros((parts, share, ff), BF), own[None], g, 0
        )

    def ordered(first, second):
        if not paired:
            return first, second
        return jnp.where(even, first, second), jnp.where(even, second, first)

    x = x_all.astype(F32)
    inverse_all = lax.rsqrt(jnp.mean(x * x, axis=1, keepdims=True) + EPS)
    normed_one = (x * inverse_all * gain_one).astype(BF)
    qkv = matmul(normed_one, qkv_full)
    attended, kept, logsum = by_group(
        forward_kernel,
        total,
        cores,
        [qkv, cosine, sine, marks_column, marks_row],
        [
            jax.ShapeDtypeStruct((cores * total, qw), BF),
            jax.ShapeDtypeStruct((cores * total, qw + 2 * kw), BF),
            jax.ShapeDtypeStruct((cores * total, 128), F32),
        ],
    )
    x_own = x_mine.astype(F32)
    send = scatter_send(matmul(attended, out_rows))
    send, first_got, kept, attended, logsum = clock.tick(
        send, first_got, kept, attended, logsum
    )

    if paired:
        second_got.append(swap(first_got[0]))
    first_got.append([fetch(clock.now(one)) for one in sends[1]])
    own = [own_columns(w_gate, ff), own_columns(w_up, ff)]
    if paired:
        own = ordered(*own)
    first_full = fill(begin(clock.now(own[0])), first_got[0][0], 0)
    second_full = begin(clock.now(own[1]))
    mid = x_own + scatter_sum(send)
    mid, first_got, first_full, second_full = clock.tick(
        mid, first_got, first_full, second_full
    )

    inverse_two = lax.rsqrt(jnp.mean(mid * mid, axis=1, keepdims=True) + EPS)
    unit_two = mid * inverse_two
    if paired:
        second_got.append(swap(first_got[1]))
    normed_two = spread((unit_two * gain_two).astype(BF))
    cot_all = spread(clock.now(cotangent[0]))
    split = share // 4 * 3
    first_full = fill(first_full, first_got[1][0], split)
    others = second_got if paired else [got[1] for got in first_got]
    second_full = fill(second_full, others[0], 0)
    normed_two, second_got, unit_two, inverse_two, first_full, second_full = clock.tick(
        normed_two, second_got, unit_two, inverse_two, first_full, second_full
    )
    normed_two = with_core(normed_two)
    cot_all = with_core(cot_all)
    others = second_got if paired else [got[1] for got in first_got]
    second_full = fill(second_full, others[1], split)
    first_full = first_full.reshape(share * parts, ff)
    second_full = second_full.reshape(share * parts, ff)
    gate, up = ordered(matmul(normed_two, first_full), matmul(normed_two, second_full))
    sigma = jax.nn.sigmoid(gate)
    active = (gate * sigma * up).astype(BF)
    grad_down = contract_first(active, cot_all).astype(BF)
    on_line = paired and cores == 2
    line = Line(clock, (share, ff))
    outs = {}

    def slot(entering, *values):
        if on_line:
            return line.slot(entering, *values)
        return clock.tick(*values) if values else None

    active, cot_all, grad_down = slot(
        (("down", 0), grad_down, (0, 0)), active, cot_all, grad_down
    )
    grad_active = contract_last(cot_all, down_rows)
    grad_gate_pre = (grad_active * up * sigma * (1.0 + gate * (1.0 - sigma))).astype(BF)
    grad_up_pre = (grad_active * gate * sigma).astype(BF)
    grad_gate_pre, grad_up_pre = slot(
        (("down", 1), grad_down, (0, 1)), grad_gate_pre, grad_up_pre
    )
    first_pre, second_pre = ordered(grad_gate_pre, grad_up_pre)
    send = scatter_send(
        contract_last(first_pre, first_full) + contract_last(second_pre, second_full)
    )
    send = slot((("down", 2), grad_down, (1, 0)), send)
    grad_normed_two = scatter_sum(send)
    grad_gate = contract_first(normed_two, clock.now(grad_gate_pre)).astype(BF)
    grad_gate = slot((("down", 3), grad_down, (1, 1)), grad_gate)
    grad_up = contract_first(normed_two, clock.now(grad_up_pre)).astype(BF)
    grad_up, grad_normed_two = slot((("gate", 0), grad_gate, (0, 0)), grad_up, grad_normed_two)
    grad_y = cotangent[0].astype(F32)
    grad_gain_two = jnp.sum(grad_normed_two * unit_two, axis=0)
    grad_mid = grad_y + norm_back(grad_normed_two, unit_two, inverse_two, gain_two)
    grad_branch = spread(grad_mid.astype(BF))
    send = scatter_send(matmul(clock.now(active), down_rows))
    grad_mid, grad_gain_two, send = slot(
        (("gate", 1), grad_gate, (1, 0)), grad_mid, grad_gain_two, send
    )
    grad_branch = slot((("gate", 2), grad_gate, (2, 0)), grad_branch)
    result = mid + scatter_sum(clock.now(send))
    grad_branch = with_core(grad_branch)
    grad_attended = contract_last(grad_branch, out_rows).astype(BF)
    grad_out = contract_first(attended, grad_branch).astype(BF)

    def both(mine):
        mine = clock.now(mine)
        return mine, from_core(mine)

    (grad_qkv,) = by_group(
        backward_kernel,
        total,
        cores,
        [kept, logsum, grad_attended, cosine, sine, marks_column, marks_row],
        [jax.ShapeDtypeStruct((cores * total, qw + 2 * kw), BF)],
        [pltpu.VMEM((total, qw + 2 * kw), F32)],
    )
    grad_qkv, grad_out, result = slot(
        (("gate", 3), grad_gate, (3, 0)), grad_qkv, grad_out, result
    )
    grad_weights = contract_first(normed_one, grad_qkv).astype(BF)
    send = scatter_send(contract_last(grad_qkv, qkv_full))
    grad_weights, send = slot((("up", 0), grad_up, (0, 0)), grad_weights, send)
    grad_normed_one = scatter_sum(send)
    if on_line:
        outs["down"] = place(
            (ff * 2, width),
            *both(line.stack("down", 4)),
            share,
            ff,
            [
                ((a * 2 + b, 0, 0), lambda k, a=a, b=b: (k * 2 + a, b))
                for a in range(2)
                for b in range(2)
            ],
        )
        grad_out = jnp.concatenate([grad_out[:, :ff], grad_out[:, ff:]], axis=0)
    outs = slot((("up", 1), grad_up, (1, 0)), outs)
    grad_normed_one, outs = slot((("up", 2), grad_up, (2, 0)), grad_normed_one, outs)
    turned = exchange(clock.now(grad_weights).reshape(parts, share, qw + 2 * kw))
    inverse_one = lax.rsqrt(jnp.mean(x_own * x_own, axis=1, keepdims=True) + EPS)
    unit_one = x_own * inverse_one
    grad_gain_one = jnp.sum(grad_normed_one * unit_one, axis=0)
    grad_x = grad_mid + norm_back(grad_normed_one, unit_one, inverse_one, gain_one)
    grad_gains = jnp.stack([grad_gain_one, grad_gain_two]).reshape(2, parts, share)
    grad_gains = jnp.sum(exchange(grad_gains.transpose(1, 0, 2)), axis=0)
    turned, grad_x = slot((("up", 3), grad_up, (3, 0)), turned, grad_x)
    turned_q = turned[:, :, :qw].transpose(1, 0, 2).reshape(share, parts * qw)
    turned_kv = turned[:, :, qw:].transpose(1, 0, 2).reshape(share, parts * 2 * kw)
    grad_gains, turned_q, turned_kv = slot(
        (("rows", 0), grad_out, (0, 0)), grad_gains, turned_q, turned_kv
    )
    if on_line:
        turned_kv = jnp.concatenate(
            [
                turned_kv,
                jnp.pad(
                    grad_gains.astype(BF), ((0, share - 2), (0, ff - parts * 2 * kw - share))
                ),
            ],
            axis=1,
        )

        def turn(name):
            return exchange(line.stack(name, parts))

        def place_columns(turned):
            return place(
                (share, ff * team),
                *both(turned),
                share,
                ff,
                [((j, 0, 0), lambda k, j=j: (0, j * 2 + k)) for j in range(parts)],
            )

        gate_turned = turn("gate")
        turned_kv = slot((("heads", 0), turned_q, (0, 0)), turned_kv)
        gate_turned = slot((("heads", 1), turned_kv, (0, 0)), gate_turned)
        outs["gate"] = place_columns(gate_turned)
        up_turned = turn("up")
        outs, up_turned = slot(None, outs, up_turned)
        outs["up"] = place_columns(up_turned)
        outs["out"] = place(
            (qw * 2, width),
            *both(line.stack("rows", 1)),
            qw,
            ff,
            [((0, b, 0), lambda k, b=b: (k, b)) for b in range(2)],
        )
        outs = slot(None, outs)
        slot(None)
        mine, other = both(line.stack("heads", 2))
        grad_gains = sum(
            one[1, :2, parts * 2 * kw : parts * 2 * kw + share].astype(F32) for one in (mine, other)
        )
        outs["query"] = place(
            (share, qw * team),
            mine,
            other,
            share,
            qw,
            [((0, 0, j), lambda k, j=j: (0, j * 2 + k)) for j in range(parts)],
        )
        narrow = [
            one[1, :, : parts * 2 * kw].reshape(share, parts, 2 * kw) for one in (mine, other)
        ]
        narrow = jnp.stack(
            [jnp.where(c == 0, *narrow), jnp.where(c == 0, *narrow[::-1])], axis=2
        ).astype(F32)
        outs["key"] = narrow[..., :kw].reshape(share, team * kw)
        outs["value"] = narrow[..., kw:].reshape(share, team * kw)
    else:
        def whole(value):
            value = lax.psum(value, "rest")[None]
            if cores == 2:
                other = from_core(value)
                value = jnp.concatenate(
                    [jnp.where(c == 0, value, other), jnp.where(c == 0, other, value)]
                )
            return value.astype(F32)

        def beside(value):
            return value.transpose(2, 1, 0, 3).reshape(share, -1)

        grad_gains = lax.psum(grad_gains, ("rest", "core"))
        outs["down"] = whole(grad_down).reshape(cores * ff, width)
        outs["out"] = whole(grad_out).reshape(cores * qw, width)
        for name, grad in (("gate", grad_gate), ("up", grad_up)):
            outs[name] = beside(whole(exchange(grad.reshape(parts, share, ff))))
        turned = whole(turned)
        outs["query"] = beside(turned[..., :qw])
        outs["key"] = beside(turned[..., qw : qw + kw])
        outs["value"] = beside(turned[..., qw + kw :])
    return (
        result.astype(BF)[None],
        grad_x.astype(BF)[None],
        grad_gains[0],
        outs["query"],
        outs["key"],
        outs["value"],
        outs["out"],
        grad_gains[1],
        outs["gate"],
        outs["up"],
        outs["down"],
    )


def solution(mesh):
    parts, replicas = mesh.devices.shape
    cores = 2 if HK % (2 * parts) == 0 and replicas % 2 == 0 else 1
    split = Mesh(
        mesh.devices.reshape(parts, replicas // cores, cores), ("group", "rest", "core")
    )
    replica = ("rest", "core")
    weights = (P("group"),) + (P("group", None),) * 4 + (P("group"),) + (P("group", None),) * 3
    split_tokens = P(replica, "group", None)
    return jax.shard_map(
        body,
        mesh=split,
        in_specs=(split_tokens, P(replica, None)) + weights + (split_tokens,),
        out_specs=(split_tokens, split_tokens) + weights,
        check_vma=False,
    )
```

```python
import jax
import jax.numpy as jnp
from jax import lax
from jax.experimental import pallas as pl
from jax.experimental.pallas import tpu as pltpu
from jax.sharding import Mesh
from jax.sharding import PartitionSpec as P

HQ = 32
HK = 8
HEAD = 64

EPS = 1e-05
BASE = 500000.0
MASKED = -1e30

BF = jnp.bfloat16
F32 = jnp.float32


def positions_of(lengths, index):
    ends = jnp.cumsum(lengths)
    starts = ends - lengths
    segment = jnp.sum((index[:, None] >= ends[None, :-1]).astype(jnp.int32), axis=1)
    member = segment[:, None] == jnp.arange(lengths.shape[0], dtype=jnp.int32)[None, :]
    start = jnp.sum(jnp.where(member, starts[None, :], 0), axis=1)
    place = jnp.where(segment == 0, index, lengths[0] + index - start)
    return (segment, place)


def matmul(left, right):
    return jnp.dot(left, right, preferred_element_type=F32)


def contract_last(left, right):
    return lax.dot_general(left, right, (((1,), (1,)), ((), ())), preferred_element_type=F32)


def contract_first(left, right):
    return lax.dot_general(left, right, (((0,), (0,)), ((), ())), preferred_element_type=F32)


def norm_back(grad_normed, unit, inverse, gain):
    scaled = grad_normed * gain
    return inverse * (scaled - unit * jnp.mean(scaled * unit, axis=1, keepdims=True))


def after(value, *others):
    return lax.optimization_barrier((value,) + others)[0]


def after(value, *others):
    return lax.optimization_barrier((value,) + others)[0]


def step_to(value, axis, step):
    size = lax.axis_size(axis)
    return lax.ppermute(value, axis, [(i, i ^ step) for i in range(size)])


def exchange(blocks):
    return lax.all_to_all(blocks, "group", 0, 0, tiled=True)


def spread(mine):
    parts = lax.axis_size("group")
    blocks = exchange(jnp.broadcast_to(mine[None], (parts,) + mine.shape))
    return blocks.reshape((parts * mine.shape[0],) + mine.shape[1:])


def from_core(value):
    return step_to(value, "core", 1)


def with_core(got):
    if lax.axis_size("core") == 1:
        return got
    return jnp.concatenate([got, from_core(got)], axis=0)


def scatter_send(partial):
    parts = lax.axis_size("group")
    if lax.axis_size("core") == 2:
        half = partial.shape[0] // 2
        partial = partial[:half] + from_core(partial[half:].astype(BF)).astype(F32)
    rows = partial.shape[0] // parts
    return partial.astype(BF).reshape((parts, rows) + partial.shape[1:])


def scatter_sum(blocks):
    return jnp.sum(exchange(blocks).astype(F32), axis=0)


def rotated(value, cosine, sine, back):
    wide = value.shape[1]
    half = HEAD // 2
    lane = lax.broadcasted_iota(jnp.int32, value.shape, 1)
    low = lane % HEAD < half
    other = jnp.where(
        low, pltpu.roll(value, wide - half, 1), pltpu.roll(value, half, 1)
    )
    sign = jnp.where(low, -1.0, 1.0)
    if back:
        sign = -sign
    return value * cosine + other * sign * sine


def visible(place_query, segment_query, place_key, segment_key):
    same = (segment_key == 0) | (segment_key == segment_query)
    return same & (place_key <= place_query)


def forward_kernel(qkv_ref, cos_ref, sin_ref, column_ref, row_ref, o_ref, kept_ref, lse_ref):
    heads = HQ // HK
    wide = heads * HEAD
    scale = HEAD ** (-0.5)
    cosine, sine = cos_ref[...], sin_ref[...]
    tiles = wide // cosine.shape[1]
    query = rotated(
        qkv_ref[:, :wide],
        jnp.concatenate([cosine] * tiles, axis=1),
        jnp.concatenate([sine] * tiles, axis=1),
        False,
    )
    query = query.astype(BF)
    pair = qkv_ref[:, wide:]
    lane = lax.broadcasted_iota(jnp.int32, pair.shape, 1)
    pair = jnp.where(lane < HEAD, rotated(pair, cosine, sine, False), pair).astype(BF)
    kept_ref[:, :wide] = query
    kept_ref[:, wide:] = pair
    key, value = pair[:, :HEAD], pair[:, HEAD:]
    allowed = visible(column_ref[:, 0:1], column_ref[:, 1:2], row_ref[0:1, :], row_ref[1:2, :])
    found = []
    for h in range(heads):
        one = query[:, h * HEAD : (h + 1) * HEAD]
        scores = jnp.where(allowed, contract_last(one, key) * scale, MASKED)
        top = jnp.max(scores, axis=1, keepdims=True)
        expo = jnp.exp(scores - top)
        denom = jnp.sum(expo, axis=1, keepdims=True)
        probs = (expo / denom).astype(BF)
        o_ref[:, h * HEAD : (h + 1) * HEAD] = matmul(probs, value).astype(BF)
        found.append(top + jnp.log(denom))
    place = lax.broadcasted_iota(jnp.int32, lse_ref.shape, 1)
    total = jnp.zeros(lse_ref.shape, F32)
    for h in range(heads):
        total = jnp.where(place == h, found[h], total)
    lse_ref[...] = total


def backward_kernel(
    kept_ref, lse_ref, grad_ref, cos_ref, sin_ref, column_ref, row_ref, out_ref, hold_ref
):
    heads = HQ // HK
    wide = heads * HEAD
    scale = HEAD ** (-0.5)
    key = kept_ref[:, wide : wide + HEAD]
    value = kept_ref[:, wide + HEAD :]
    allowed = visible(column_ref[:, 0:1], column_ref[:, 1:2], row_ref[0:1, :], row_ref[1:2, :])
    total = key.shape[0]
    grad_k = jnp.zeros((total, HEAD), F32)
    grad_v = jnp.zeros((total, HEAD), F32)
    for h in range(heads):
        one = kept_ref[:, h * HEAD : (h + 1) * HEAD]
        grad = grad_ref[:, h * HEAD : (h + 1) * HEAD]
        scores = jnp.where(allowed, contract_last(one, key) * scale, MASKED)
        probs = jnp.exp(scores - lse_ref[:, h : h + 1])
        grad_p = contract_last(grad, value)
        grad_s = probs * (grad_p - jnp.sum(probs * grad_p, axis=1, keepdims=True))
        grad_s = grad_s.astype(BF)
        hold_ref[:, h * HEAD : (h + 1) * HEAD] = matmul(grad_s, key) * scale
        grad_k = grad_k + contract_first(grad_s, one)
        grad_v = grad_v + contract_first(probs.astype(BF), grad)
    hold_ref[:, wide : wide + HEAD] = grad_k * scale
    hold_ref[:, wide + HEAD :] = grad_v
    cosine, sine = cos_ref[...], sin_ref[...]
    tiles = wide // cosine.shape[1]
    out_ref[:, :wide] = rotated(
        hold_ref[:, :wide],
        jnp.concatenate([cosine] * tiles, axis=1),
        jnp.concatenate([sine] * tiles, axis=1),
        True,
    ).astype(BF)
    pair = hold_ref[:, wide:]
    lane = lax.broadcasted_iota(jnp.int32, pair.shape, 1)
    pair = jnp.where(lane < HEAD, rotated(pair, cosine, sine, True), pair)
    out_ref[:, wide:] = pair.astype(BF)


def by_group(kernel, total, groups, inputs, outputs, scratch=()):
    def spec(shape):
        if len(shape) == 3:
            return pl.BlockSpec((None,) + shape[1:], lambda i: (i, 0, 0))
        return pl.BlockSpec((total, shape[1]), lambda i: (i, 0))

    return pl.pallas_call(
        kernel,
        grid=(groups,),
        in_specs=[spec(one.shape) for one in inputs],
        out_specs=[spec(one.shape) for one in outputs],
        out_shape=list(outputs),
        scratch_shapes=list(scratch),
        compiler_params=pltpu.CompilerParams(vmem_limit_bytes=40 * 2**20),
        cost_estimate=pl.CostEstimate(flops=0, bytes_accessed=1, transcendentals=0),
    )(*inputs)


class Clock:
    def __init__(self):
        self.token = jnp.zeros((8, 128), F32)

    def tick(self, *values):
        flat, tree = jax.tree.flatten(values)
        out = lax.optimization_barrier((self.token, *flat))
        self.token = out[0]
        values = jax.tree.unflatten(tree, out[1:])
        return values[0] if len(values) == 1 else values

    def now(self, value):
        return after(value, self.token)


class Line:
    def __init__(self, clock, shape):
        self.clock = clock
        self.shape = shape
        place = lax.axis_index("rest")
        self.inner = (place == 1) | (place == 2)
        self.sums = {}
        self.flight = {}

    def piece(self, array, block):
        rows, wide = self.shape
        if array.ndim == 3:
            return array[block[0]]
        row, column = block
        return array[row * rows : (row + 1) * rows, column * wide : (column + 1) * wide]

    def slot(self, entering, *values):
        last = self.flight
        came, moved, values = self.clock.tick(last.get("came"), last.get("moved"), values)
        if entering is not None:
            name, array, block = entering
            entering = (name, self.clock.now(array), block)
        part, send = self.combine(last, came, moved, entering)
        across = last["enter"][0] if part is not None else None
        flight = {"enter": entering, "across": across, "part": part}
        if last.get("across"):
            flight["out"] = (last["across"], send)
        if part is not None:
            flight["moved"] = lax.ppermute(part, "rest", [(1, 2), (2, 1)])
        if send is not None:
            flight["came"] = lax.ppermute(send, "rest", [(0, 1), (1, 0), (2, 3), (3, 2)])
        if last.get("out"):
            name, full = last["out"]
            self.sums[name] = (full, came)
        self.flight = flight
        return values[0] if len(values) == 1 else values

    def stack(self, name, count):
        rows, wide = self.shape
        steps = 2
        tile = rows // steps
        pairs = [self.sums[name, k] for k in range(count)]

        def spec(k, used):
            def at(j, i, w):
                here = jnp.where(j == k, i, jnp.where(j < k, 0, steps - 1))
                return (jnp.where(w[0] == used, here, 0), 0)

            return pl.BlockSpec((tile, wide), at)

        def kernel(where_ref, *refs):
            for k in range(count):
                for used in range(2):

                    @pl.when((pl.program_id(0) == k) & (where_ref[0] == used))
                    def _(k=k, used=used):
                        refs[-1][...] = refs[2 * k + 1 - used][...]

        return pl.pallas_call(
            kernel,
            grid_spec=pltpu.PrefetchScalarGridSpec(
                num_scalar_prefetch=1,
                grid=(count, steps),
                in_specs=[spec(k, used) for k in range(count) for used in (1, 0)],
                out_specs=pl.BlockSpec((None, tile, wide), lambda j, i, w: (j, i, 0)),
            ),
            out_shape=jax.ShapeDtypeStruct((count, rows, wide), BF),
            compiler_params=pltpu.CompilerParams(vmem_limit_bytes=16 * 2**20),
            cost_estimate=pl.CostEstimate(flops=0, bytes_accessed=1, transcendentals=0),
        )(self.inner.astype(jnp.int32)[None], *[one for pair in pairs for one in pair])

    def combine(self, stream, came, moved, entering):
        rows, wide = self.shape
        steps = 4
        tile = rows // steps
        last, across = stream.get("enter"), stream.get("across")

        def spec(block, used):
            def at(i, w):
                here = jnp.where(w[0] == used, i, 0)
                return block[:-2] + (block[-2] * steps + here, block[-1])

            return pl.BlockSpec((None,) * (len(block) - 2) + (tile, wide), at)

        inputs, names = [], []

        def take(name, array, block, used):
            inputs.append((array, spec(block, used)))
            names.append(name)

        if last is not None:
            take("came", came, (0, 0), 1)
            take("last", last[1], last[2], 1)
        if across is not None:
            take("part", stream["part"], (0, 0), 1)
            take("moved", moved, (0, 0), 1)
        if entering is not None:
            take("next", entering[1], entering[2], 0)
        given = []
        if last is not None:
            given.append("part")
        if across is not None or entering is not None:
            given.append("send")
        if not given:
            return None, None

        def kernel(where_ref, *refs):
            read = dict(zip(names, refs))
            write = dict(zip(given, refs[len(names) :]))

            @pl.when(where_ref[0] == 1)
            def _():
                if "last" in read:
                    total = read["last"][...].astype(F32) + read["came"][...].astype(F32)
                    write["part"][...] = total.astype(BF)
                if "part" in read:
                    total = read["part"][...].astype(F32) + read["moved"][...].astype(F32)
                    write["send"][...] = total.astype(BF)

            if "next" in read:

                @pl.when(where_ref[0] == 0)
                def _():
                    write["send"][...] = read["next"][...]

        results = pl.pallas_call(
            kernel,
            grid_spec=pltpu.PrefetchScalarGridSpec(
                num_scalar_prefetch=1,
                grid=(steps,),
                in_specs=[one[1] for one in inputs],
                out_specs=[
                    pl.BlockSpec(
                        (tile, wide),
                        lambda i, w: (i, 0)
                        if name == "send"
                        else (jnp.where(w[0] == 1, i, 0), 0),
                    )
                    for name in given
                ],
            ),
            out_shape=[jax.ShapeDtypeStruct((rows, wide), BF)] * len(given),
            compiler_params=pltpu.CompilerParams(vmem_limit_bytes=16 * 2**20),
            cost_estimate=pl.CostEstimate(flops=0, bytes_accessed=1, transcendentals=0),
        )(self.inner.astype(jnp.int32)[None], *[one[0] for one in inputs])
        results = dict(zip(given, results))
        return results.get("part"), results.get("send")


def place(shape, mine, other, rows, wide, blocks):
    core = lax.axis_index("core")
    table = jnp.asarray(
        [[list(there) + list(here(k)) for k in range(2)] for there, here in blocks], jnp.int32
    )
    table = jnp.stack([table[:, 0], table[:, 1]])
    table = jnp.where(core == 0, table, table[::-1])
    count = len(blocks)
    table = table.reshape(-1)
    size = table.shape[0] // (2 * count)

    def entry(w, k, j, field):
        return w[(k * count + j) * size + field]

    def source(k, j, w, own):
        j = jnp.where(k == own, j, count - 1 if own == 0 else 0)
        return tuple(entry(w, k, j, field) for field in range(3))

    def kernel(table_ref, mine_ref, other_ref, out_ref):
        @pl.when(pl.program_id(0) == 0)
        def _():
            out_ref[...] = mine_ref[...].astype(F32)

        @pl.when(pl.program_id(0) == 1)
        def _():
            out_ref[...] = other_ref[...].astype(F32)

    return pl.pallas_call(
        kernel,
        grid_spec=pltpu.PrefetchScalarGridSpec(
            num_scalar_prefetch=1,
            grid=(2, count),
            in_specs=[
                pl.BlockSpec((None, rows, wide), lambda k, j, w: source(k, j, w, 0)),
                pl.BlockSpec((None, rows, wide), lambda k, j, w: source(k, j, w, 1)),
            ],
            out_specs=pl.BlockSpec(
                (rows, wide), lambda k, j, w: (entry(w, k, j, 3), entry(w, k, j, 4))
            ),
        ),
        out_shape=jax.ShapeDtypeStruct(shape, F32),
        compiler_params=pltpu.CompilerParams(vmem_limit_bytes=16 * 2**20),
        cost_estimate=pl.CostEstimate(
            flops=0, bytes_accessed=12 * count * rows * wide, transcendentals=0
        ),
    )(table, mine, other)


def body(
    tokens,
    seq_lengths,
    attn_gain,
    w_query,
    w_key,
    w_value,
    w_out,
    mlp_gain,
    w_gate,
    w_up,
    w_down,
    cotangent,
):
    parts = lax.axis_size("group")
    cores = lax.axis_size("core")
    g = lax.axis_index("group")
    c = lax.axis_index("core")
    rows, width = tokens.shape[1:]
    total = rows * parts
    team = parts * cores
    heads = HQ // HK
    scale = HEAD ** (-0.5)
    ff = w_gate.shape[1] // team
    share = w_gate.shape[0]
    qw = HQ * HEAD // team
    kw = HK * HEAD // team
    assert kw == HEAD

    def columns(weight, size, rows=slice(None)):
        return jnp.stack(
            [
                lax.dynamic_slice_in_dim(weight[rows], (k * cores + c) * size, size, 1)
                for k in range(parts)
            ]
        )

    def fetch(blocks):
        return [
            step_to(lax.dynamic_index_in_dim(blocks, g ^ s, 0, keepdims=False), "group", s)
            for s in range(1, parts)
        ]

    def in_order(own, got):
        out = jnp.zeros((parts,) + own.shape, own.dtype)
        for s, block in enumerate([own] + got):
            out = lax.dynamic_update_slice_in_dim(out, block[None], g ^ s, 0)
        return out.reshape((parts * own.shape[0],) + own.shape[1:])

    def own_columns(weight, size):
        return lax.dynamic_slice_in_dim(weight, (g * cores + c) * size, size, 1)

    clock = Clock()
    x_mine = tokens[0]
    extra = 2 * share // width if 2 * share > width else 1
    gains = jnp.concatenate([attn_gain, mlp_gain])
    gains = jnp.pad(gains, (0, 16 * width - gains.shape[0])).reshape(16, width)
    x_got = spread(jnp.concatenate([x_mine, gains], axis=0))
    x_got = x_got.reshape(parts, rows + 16, width)
    gains = x_got[:, rows].reshape(parts, width)[:, : 2 * share]
    gain_one = gains[:, :share].reshape(-1).astype(F32)
    gain_two = gains[:, share:].reshape(-1).astype(F32)
    x_got = x_got[:, :rows].reshape(parts * rows, width)
    qkv_send = jnp.concatenate(
        [columns(w_query, qw), columns(w_key, kw), columns(w_value, kw)], axis=2
    )
    qkv_got = fetch(qkv_send)
    qkv_own = lax.dynamic_index_in_dim(qkv_send, g, 0, keepdims=False)

    paired = lax.axis_size("rest") == 4
    even = lax.axis_index("rest") % 2 == 0
    halves = [slice(0, share // 4 * 3), slice(share // 4 * 3, share)]
    sends = []
    for half in halves:
        gate_send = columns(w_gate, ff, half)
        up_send = columns(w_up, ff, half)
        sends.append([jnp.where(even, gate_send, up_send)] if paired else [gate_send, up_send])
    lengths = [seq_lengths[0]]
    if cores == 2:
        lengths.append(from_core(seq_lengths[0]))
    index = jnp.arange(total, dtype=jnp.int32)
    marks = [positions_of(one, index) for one in lengths]
    half = HEAD // 2
    freq = BASE ** (-(2.0 * jnp.arange(half, dtype=F32)) / HEAD)
    place_all = jnp.concatenate([one[1] for one in marks]).astype(F32)
    angle = place_all[:, None] * jnp.tile(freq, 128 // half)[None, :]
    cosine, sine = jnp.cos(angle), jnp.sin(angle)
    marks_row = jnp.stack([jnp.stack([one[1], one[0]]) for one in marks])
    marks_column = marks_row.transpose(0, 2, 1)
    x_got, qkv_got, sends, cosine, sine, marks_row, marks_column = clock.tick(
        x_got, qkv_got, sends, cosine, sine, marks_row, marks_column
    )

    out_rows = lax.dynamic_slice_in_dim(w_out, c * qw, qw, 0)
    down_rows = lax.dynamic_slice_in_dim(w_down, c * ff, ff, 0)
    first_got = [[fetch(one) for one in sends[0]]]
    second_got = []
    qkv_full = in_order(qkv_own, qkv_got)
    x_all = with_core(x_got)

    def swap(got):
        return step_to(jnp.stack(got[0]), "rest", 1)

    def fill(out, got, row):
        for s in range(1, parts):
            out = lax.dynamic_update_slice(out, got[s - 1][None], (g ^ s, row, 0))
        return out

    def begin(own):
        return lax.dynamic_update_slice_in_dim(
            jnp.zeros((parts, share, ff), BF), own[None], g, 0
        )

    def ordered(first, second):
        if not paired:
            return first, second
        return jnp.where(even, first, second), jnp.where(even, second, first)

    x = x_all.astype(F32)
    inverse_all = lax.rsqrt(jnp.mean(x * x, axis=1, keepdims=True) + EPS)
    normed_one = (x * inverse_all * gain_one).astype(BF)
    qkv = matmul(normed_one, qkv_full)
    attended, kept, logsum = by_group(
        forward_kernel,
        total,
        cores,
        [qkv, cosine, sine, marks_column, marks_row],
        [
            jax.ShapeDtypeStruct((cores * total, qw), BF),
            jax.ShapeDtypeStruct((cores * total, qw + 2 * kw), BF),
            jax.ShapeDtypeStruct((cores * total, 128), F32),
        ],
    )
    x_own = x_mine.astype(F32)
    send = scatter_send(matmul(attended, out_rows))
    send, first_got, kept, attended, logsum = clock.tick(
        send, first_got, kept, attended, logsum
    )

    if paired:
        second_got.append(swap(first_got[0]))
    first_got.append([fetch(clock.now(one)) for one in sends[1]])
    own = [own_columns(w_gate, ff), own_columns(w_up, ff)]
    if paired:
        own = ordered(*own)
    first_full = fill(begin(clock.now(own[0])), first_got[0][0], 0)
    second_full = begin(clock.now(own[1]))
    mid = x_own + scatter_sum(send)
    mid, first_got, first_full, second_full = clock.tick(
        mid, first_got, first_full, second_full
    )

    inverse_two = lax.rsqrt(jnp.mean(mid * mid, axis=1, keepdims=True) + EPS)
    unit_two = mid * inverse_two
    if paired:
        second_got.append(swap(first_got[1]))
    normed_two = spread((unit_two * gain_two).astype(BF))
    cot_all = spread(clock.now(cotangent[0]))
    split = share // 4 * 3
    first_full = fill(first_full, first_got[1][0], split)
    others = second_got if paired else [got[1] for got in first_got]
    second_full = fill(second_full, others[0], 0)
    normed_two, second_got, unit_two, inverse_two, first_full, second_full = clock.tick(
        normed_two, second_got, unit_two, inverse_two, first_full, second_full
    )
    normed_two = with_core(normed_two)
    cot_all = with_core(cot_all)
    others = second_got if paired else [got[1] for got in first_got]
    second_full = fill(second_full, others[1], split)
    first_full = first_full.reshape(share * parts, ff)
    second_full = second_full.reshape(share * parts, ff)
    gate, up = ordered(matmul(normed_two, first_full), matmul(normed_two, second_full))
    sigma = jax.nn.sigmoid(gate)
    active = (gate * sigma * up).astype(BF)
    grad_down = contract_first(active, cot_all).astype(BF)
    on_line = paired and cores == 2
    line = Line(clock, (share, ff))
    outs = {}

    def slot(entering, *values):
        if on_line:
            return line.slot(entering, *values)
        return clock.tick(*values) if values else None

    active, cot_all, grad_down = slot(
        (("down", 0), grad_down, (0, 0)), active, cot_all, grad_down
    )
    grad_active = contract_last(cot_all, down_rows)
    grad_gate_pre = (grad_active * up * sigma * (1.0 + gate * (1.0 - sigma))).astype(BF)
    grad_up_pre = (grad_active * gate * sigma).astype(BF)
    grad_gate_pre, grad_up_pre = slot(
        (("down", 1), grad_down, (0, 1)), grad_gate_pre, grad_up_pre
    )
    first_pre, second_pre = ordered(grad_gate_pre, grad_up_pre)
    send = scatter_send(
        contract_last(first_pre, first_full) + contract_last(second_pre, second_full)
    )
    send = slot((("down", 2), grad_down, (1, 0)), send)
    grad_normed_two = scatter_sum(send)
    grad_gate = contract_first(normed_two, clock.now(grad_gate_pre)).astype(BF)
    grad_gate = slot((("down", 3), grad_down, (1, 1)), grad_gate)
    grad_up = contract_first(normed_two, clock.now(grad_up_pre)).astype(BF)
    grad_up, grad_normed_two = slot((("gate", 0), grad_gate, (0, 0)), grad_up, grad_normed_two)
    grad_y = cotangent[0].astype(F32)
    grad_gain_two = jnp.sum(grad_normed_two * unit_two, axis=0)
    grad_mid = grad_y + norm_back(grad_normed_two, unit_two, inverse_two, gain_two)
    grad_branch = spread(grad_mid.astype(BF))
    send = scatter_send(matmul(clock.now(active), down_rows))
    grad_mid, grad_gain_two, send = slot(
        (("gate", 1), grad_gate, (1, 0)), grad_mid, grad_gain_two, send
    )
    grad_branch = slot((("gate", 2), grad_gate, (2, 0)), grad_branch)
    result = mid + scatter_sum(clock.now(send))
    grad_branch = with_core(grad_branch)
    grad_attended = contract_last(grad_branch, out_rows).astype(BF)
    grad_out = contract_first(attended, grad_branch).astype(BF)

    def both(mine):
        mine = clock.now(mine)
        return mine, from_core(mine)

    (grad_qkv,) = by_group(
        backward_kernel,
        total,
        cores,
        [kept, logsum, grad_attended, cosine, sine, marks_column, marks_row],
        [jax.ShapeDtypeStruct((cores * total, qw + 2 * kw), BF)],
        [pltpu.VMEM((total, qw + 2 * kw), F32)],
    )
    grad_qkv, grad_out, result = slot(
        (("gate", 3), grad_gate, (3, 0)), grad_qkv, grad_out, result
    )
    grad_weights = contract_first(normed_one, grad_qkv).astype(BF)
    send = scatter_send(contract_last(grad_qkv, qkv_full))
    grad_weights, send = slot((("up", 0), grad_up, (0, 0)), grad_weights, send)
    grad_normed_one = scatter_sum(send)
    if on_line:
        outs["down"] = place(
            (ff * 2, width),
            *both(line.stack("down", 4)),
            share,
            ff,
            [
                ((a * 2 + b, 0, 0), lambda k, a=a, b=b: (k * 2 + a, b))
                for a in range(2)
                for b in range(2)
            ],
        )
        grad_out = jnp.concatenate([grad_out[:, :ff], grad_out[:, ff:]], axis=0)
    outs = slot((("up", 1), grad_up, (1, 0)), outs)
    grad_normed_one, outs = slot((("up", 2), grad_up, (2, 0)), grad_normed_one, outs)
    turned = exchange(clock.now(grad_weights).reshape(parts, share, qw + 2 * kw))
    inverse_one = lax.rsqrt(jnp.mean(x_own * x_own, axis=1, keepdims=True) + EPS)
    unit_one = x_own * inverse_one
    grad_gain_one = jnp.sum(grad_normed_one * unit_one, axis=0)
    grad_x = grad_mid + norm_back(grad_normed_one, unit_one, inverse_one, gain_one)
    grad_gains = jnp.stack([grad_gain_one, grad_gain_two]).reshape(2, parts, share)
    grad_gains = jnp.sum(exchange(grad_gains.transpose(1, 0, 2)), axis=0)
    turned, grad_x = slot((("up", 3), grad_up, (3, 0)), turned, grad_x)
    turned_q = turned[:, :, :qw].transpose(1, 0, 2).reshape(share, parts * qw)
    turned_kv = turned[:, :, qw:].transpose(1, 0, 2).reshape(share, parts * 2 * kw)
    grad_gains, turned_q, turned_kv = slot(
        (("heads", 0), turned_q, (0, 0)), grad_gains, turned_q, turned_kv
    )
    if on_line:
        turned_kv = jnp.concatenate(
            [
                turned_kv,
                jnp.pad(
                    grad_gains.astype(BF), ((0, share - 2), (0, ff - parts * 2 * kw - share))
                ),
            ],
            axis=1,
        )

        def turn(name):
            return exchange(line.stack(name, parts))

        def place_columns(turned):
            return place(
                (share, ff * team),
                *both(turned),
                share,
                ff,
                [((j, 0, 0), lambda k, j=j: (0, j * 2 + k)) for j in range(parts)],
            )

        gate_turned = turn("gate")
        turned_kv = slot((("heads", 1), turned_kv, (0, 0)), turned_kv)
        gate_turned = slot((("rows", 0), grad_out, (0, 0)), gate_turned)
        outs["gate"] = place_columns(gate_turned)
        up_turned = turn("up")
        outs, up_turned = slot(None, outs, up_turned)
        outs["up"] = place_columns(up_turned)
        outs = slot(None, outs)
        mine, other = both(line.stack("heads", 2))
        grad_gains = sum(
            one[1, :2, parts * 2 * kw : parts * 2 * kw + share].astype(F32) for one in (mine, other)
        )
        outs["query"] = place(
            (share, qw * team),
            mine,
            other,
            share,
            qw,
            [((0, 0, j), lambda k, j=j: (0, j * 2 + k)) for j in range(parts)],
        )
        narrow = [
            one[1, :, : parts * 2 * kw].reshape(share, parts, 2 * kw) for one in (mine, other)
        ]
        narrow = jnp.stack(
            [jnp.where(c == 0, *narrow), jnp.where(c == 0, *narrow[::-1])], axis=2
        ).astype(F32)
        outs["key"] = narrow[..., :kw].reshape(share, team * kw)
        outs["value"] = narrow[..., kw:].reshape(share, team * kw)
        outs = slot(None, outs)
        outs["out"] = place(
            (qw * 2, width),
            *both(line.stack("rows", 1)),
            qw,
            ff,
            [((0, b, 0), lambda k, b=b: (k, b)) for b in range(2)],
        )
    else:
        def whole(value):
            value = lax.psum(value, "rest")[None]
            if cores == 2:
                other = from_core(value)
                value = jnp.concatenate(
                    [jnp.where(c == 0, value, other), jnp.where(c == 0, other, value)]
                )
            return value.astype(F32)

        def beside(value):
            return value.transpose(2, 1, 0, 3).reshape(share, -1)

        grad_gains = lax.psum(grad_gains, ("rest", "core"))
        outs["down"] = whole(grad_down).reshape(cores * ff, width)
        outs["out"] = whole(grad_out).reshape(cores * qw, width)
        for name, grad in (("gate", grad_gate), ("up", grad_up)):
            outs[name] = beside(whole(exchange(grad.reshape(parts, share, ff))))
        turned = whole(turned)
        outs["query"] = beside(turned[..., :qw])
        outs["key"] = beside(turned[..., qw : qw + kw])
        outs["value"] = beside(turned[..., qw + kw :])
    return (
        result.astype(BF)[None],
        grad_x.astype(BF)[None],
        grad_gains[0],
        outs["query"],
        outs["key"],
        outs["value"],
        outs["out"],
        grad_gains[1],
        outs["gate"],
        outs["up"],
        outs["down"],
    )


def solution(mesh):
    parts, replicas = mesh.devices.shape
    cores = 2 if HK % (2 * parts) == 0 and replicas % 2 == 0 else 1
    split = Mesh(
        mesh.devices.reshape(parts, replicas // cores, cores), ("group", "rest", "core")
    )
    replica = ("rest", "core")
    weights = (P("group"),) + (P("group", None),) * 4 + (P("group"),) + (P("group", None),) * 3
    split_tokens = P(replica, "group", None)
    return jax.shard_map(
        body,
        mesh=split,
        in_specs=(split_tokens, P(replica, None)) + weights + (split_tokens,),
        out_specs=(split_tokens, split_tokens) + weights,
        check_vma=False,
    )
```

```python
import jax
import jax.numpy as jnp
from jax import lax
from jax.experimental import pallas as pl
from jax.experimental.pallas import tpu as pltpu
from jax.sharding import Mesh
from jax.sharding import PartitionSpec as P

HQ = 32
HK = 8
HEAD = 64

EPS = 1e-05
BASE = 500000.0
MASKED = -1e30

BF = jnp.bfloat16
F32 = jnp.float32


def positions_of(lengths, index):
    ends = jnp.cumsum(lengths)
    starts = ends - lengths
    segment = jnp.sum((index[:, None] >= ends[None, :-1]).astype(jnp.int32), axis=1)
    member = segment[:, None] == jnp.arange(lengths.shape[0], dtype=jnp.int32)[None, :]
    start = jnp.sum(jnp.where(member, starts[None, :], 0), axis=1)
    place = jnp.where(segment == 0, index, lengths[0] + index - start)
    return (segment, place)


def matmul(left, right):
    return jnp.dot(left, right, preferred_element_type=F32)


def contract_last(left, right):
    return lax.dot_general(left, right, (((1,), (1,)), ((), ())), preferred_element_type=F32)


def contract_first(left, right):
    return lax.dot_general(left, right, (((0,), (0,)), ((), ())), preferred_element_type=F32)


def norm_back(grad_normed, unit, inverse, gain):
    scaled = grad_normed * gain
    return inverse * (scaled - unit * jnp.mean(scaled * unit, axis=1, keepdims=True))


def after(value, *others):
    return lax.optimization_barrier((value,) + others)[0]


def after(value, *others):
    return lax.optimization_barrier((value,) + others)[0]


def step_to(value, axis, step):
    size = lax.axis_size(axis)
    return lax.ppermute(value, axis, [(i, i ^ step) for i in range(size)])


def exchange(blocks):
    return lax.all_to_all(blocks, "group", 0, 0, tiled=True)


def spread(mine):
    parts = lax.axis_size("group")
    blocks = exchange(jnp.broadcast_to(mine[None], (parts,) + mine.shape))
    return blocks.reshape((parts * mine.shape[0],) + mine.shape[1:])


def from_core(value):
    return step_to(value, "core", 1)


def with_core(got):
    if lax.axis_size("core") == 1:
        return got
    return jnp.concatenate([got, from_core(got)], axis=0)


def scatter_send(partial):
    parts = lax.axis_size("group")
    if lax.axis_size("core") == 2:
        half = partial.shape[0] // 2
        partial = partial[:half] + from_core(partial[half:].astype(BF)).astype(F32)
    rows = partial.shape[0] // parts
    return partial.astype(BF).reshape((parts, rows) + partial.shape[1:])


def scatter_sum(blocks):
    return jnp.sum(exchange(blocks).astype(F32), axis=0)


def rotated(value, cosine, sine, back):
    wide = value.shape[1]
    half = HEAD // 2
    lane = lax.broadcasted_iota(jnp.int32, value.shape, 1)
    low = lane % HEAD < half
    other = jnp.where(
        low, pltpu.roll(value, wide - half, 1), pltpu.roll(value, half, 1)
    )
    sign = jnp.where(low, -1.0, 1.0)
    if back:
        sign = -sign
    return value * cosine + other * sign * sine


def visible(place_query, segment_query, place_key, segment_key):
    same = (segment_key == 0) | (segment_key == segment_query)
    return same & (place_key <= place_query)


def forward_kernel(qkv_ref, cos_ref, sin_ref, column_ref, row_ref, o_ref, kept_ref, lse_ref):
    heads = HQ // HK
    wide = heads * HEAD
    scale = HEAD ** (-0.5)
    cosine, sine = cos_ref[...], sin_ref[...]
    tiles = wide // cosine.shape[1]
    query = rotated(
        qkv_ref[:, :wide],
        jnp.concatenate([cosine] * tiles, axis=1),
        jnp.concatenate([sine] * tiles, axis=1),
        False,
    )
    query = query.astype(BF)
    pair = qkv_ref[:, wide:]
    lane = lax.broadcasted_iota(jnp.int32, pair.shape, 1)
    pair = jnp.where(lane < HEAD, rotated(pair, cosine, sine, False), pair).astype(BF)
    kept_ref[:, :wide] = query
    kept_ref[:, wide:] = pair
    key, value = pair[:, :HEAD], pair[:, HEAD:]
    allowed = visible(column_ref[:, 0:1], column_ref[:, 1:2], row_ref[0:1, :], row_ref[1:2, :])
    found = []
    for h in range(heads):
        one = query[:, h * HEAD : (h + 1) * HEAD]
        scores = jnp.where(allowed, contract_last(one, key) * scale, MASKED)
        top = jnp.max(scores, axis=1, keepdims=True)
        expo = jnp.exp(scores - top)
        denom = jnp.sum(expo, axis=1, keepdims=True)
        probs = (expo / denom).astype(BF)
        o_ref[:, h * HEAD : (h + 1) * HEAD] = matmul(probs, value).astype(BF)
        found.append(top + jnp.log(denom))
    place = lax.broadcasted_iota(jnp.int32, lse_ref.shape, 1)
    total = jnp.zeros(lse_ref.shape, F32)
    for h in range(heads):
        total = jnp.where(place == h, found[h], total)
    lse_ref[...] = total


def backward_kernel(
    kept_ref, lse_ref, grad_ref, cos_ref, sin_ref, column_ref, row_ref, out_ref, hold_ref
):
    heads = HQ // HK
    wide = heads * HEAD
    scale = HEAD ** (-0.5)
    key = kept_ref[:, wide : wide + HEAD]
    value = kept_ref[:, wide + HEAD :]
    allowed = visible(column_ref[:, 0:1], column_ref[:, 1:2], row_ref[0:1, :], row_ref[1:2, :])
    total = key.shape[0]
    grad_k = jnp.zeros((total, HEAD), F32)
    grad_v = jnp.zeros((total, HEAD), F32)
    for h in range(heads):
        one = kept_ref[:, h * HEAD : (h + 1) * HEAD]
        grad = grad_ref[:, h * HEAD : (h + 1) * HEAD]
        scores = jnp.where(allowed, contract_last(one, key) * scale, MASKED)
        probs = jnp.exp(scores - lse_ref[:, h : h + 1])
        grad_p = contract_last(grad, value)
        grad_s = probs * (grad_p - jnp.sum(probs * grad_p, axis=1, keepdims=True))
        grad_s = grad_s.astype(BF)
        hold_ref[:, h * HEAD : (h + 1) * HEAD] = matmul(grad_s, key) * scale
        grad_k = grad_k + contract_first(grad_s, one)
        grad_v = grad_v + contract_first(probs.astype(BF), grad)
    hold_ref[:, wide : wide + HEAD] = grad_k * scale
    hold_ref[:, wide + HEAD :] = grad_v
    cosine, sine = cos_ref[...], sin_ref[...]
    tiles = wide // cosine.shape[1]
    out_ref[:, :wide] = rotated(
        hold_ref[:, :wide],
        jnp.concatenate([cosine] * tiles, axis=1),
        jnp.concatenate([sine] * tiles, axis=1),
        True,
    ).astype(BF)
    pair = hold_ref[:, wide:]
    lane = lax.broadcasted_iota(jnp.int32, pair.shape, 1)
    pair = jnp.where(lane < HEAD, rotated(pair, cosine, sine, True), pair)
    out_ref[:, wide:] = pair.astype(BF)


def by_group(kernel, total, groups, inputs, outputs, scratch=()):
    def spec(shape):
        if len(shape) == 3:
            return pl.BlockSpec((None,) + shape[1:], lambda i: (i, 0, 0))
        return pl.BlockSpec((total, shape[1]), lambda i: (i, 0))

    return pl.pallas_call(
        kernel,
        grid=(groups,),
        in_specs=[spec(one.shape) for one in inputs],
        out_specs=[spec(one.shape) for one in outputs],
        out_shape=list(outputs),
        scratch_shapes=list(scratch),
        compiler_params=pltpu.CompilerParams(vmem_limit_bytes=40 * 2**20),
        cost_estimate=pl.CostEstimate(flops=0, bytes_accessed=1, transcendentals=0),
    )(*inputs)


class Clock:
    def __init__(self):
        self.token = jnp.zeros((8, 128), F32)

    def tick(self, *values):
        flat, tree = jax.tree.flatten(values)
        out = lax.optimization_barrier((self.token, *flat))
        self.token = out[0]
        values = jax.tree.unflatten(tree, out[1:])
        return values[0] if len(values) == 1 else values

    def now(self, value):
        return after(value, self.token)


class Line:
    def __init__(self, clock, shape):
        self.clock = clock
        self.shape = shape
        place = lax.axis_index("rest")
        self.inner = (place == 1) | (place == 2)
        self.sums = {}
        self.flight = {}

    def piece(self, array, block):
        rows, wide = self.shape
        if array.ndim == 3:
            return array[block[0]]
        row, column = block
        return array[row * rows : (row + 1) * rows, column * wide : (column + 1) * wide]

    def slot(self, entering, *values):
        last = self.flight
        came, moved, values = self.clock.tick(last.get("came"), last.get("moved"), values)
        if entering is not None:
            name, array, block = entering
            entering = (name, self.clock.now(array), block)
        part, send = self.combine(last, came, moved, entering)
        across = last["enter"][0] if part is not None else None
        flight = {"enter": entering, "across": across, "part": part}
        if last.get("across"):
            flight["out"] = (last["across"], send)
        if part is not None:
            flight["moved"] = lax.ppermute(part, "rest", [(1, 2), (2, 1)])
        if send is not None:
            flight["came"] = lax.ppermute(send, "rest", [(0, 1), (1, 0), (2, 3), (3, 2)])
        if last.get("out"):
            name, full = last["out"]
            self.sums[name] = (full, came)
        self.flight = flight
        return values[0] if len(values) == 1 else values

    def stack(self, name, count):
        rows, wide = self.shape
        steps = 2
        tile = rows // steps
        pairs = [self.sums[name, k] for k in range(count)]

        def spec(k, used):
            def at(j, i, w):
                here = jnp.where(j == k, i, jnp.where(j < k, 0, steps - 1))
                return (jnp.where(w[0] == used, here, 0), 0)

            return pl.BlockSpec((tile, wide), at)

        def kernel(where_ref, *refs):
            for k in range(count):
                for used in range(2):

                    @pl.when((pl.program_id(0) == k) & (where_ref[0] == used))
                    def _(k=k, used=used):
                        refs[-1][...] = refs[2 * k + 1 - used][...]

        return pl.pallas_call(
            kernel,
            grid_spec=pltpu.PrefetchScalarGridSpec(
                num_scalar_prefetch=1,
                grid=(count, steps),
                in_specs=[spec(k, used) for k in range(count) for used in (1, 0)],
                out_specs=pl.BlockSpec((None, tile, wide), lambda j, i, w: (j, i, 0)),
            ),
            out_shape=jax.ShapeDtypeStruct((count, rows, wide), BF),
            compiler_params=pltpu.CompilerParams(vmem_limit_bytes=16 * 2**20),
            cost_estimate=pl.CostEstimate(flops=0, bytes_accessed=1, transcendentals=0),
        )(self.inner.astype(jnp.int32)[None], *[one for pair in pairs for one in pair])

    def combine(self, stream, came, moved, entering):
        rows, wide = self.shape
        steps = 4
        tile = rows // steps
        last, across = stream.get("enter"), stream.get("across")

        def spec(block, used):
            def at(i, w):
                here = jnp.where(w[0] == used, i, 0)
                return block[:-2] + (block[-2] * steps + here, block[-1])

            return pl.BlockSpec((None,) * (len(block) - 2) + (tile, wide), at)

        inputs, names = [], []

        def take(name, array, block, used):
            inputs.append((array, spec(block, used)))
            names.append(name)

        if last is not None:
            take("came", came, (0, 0), 1)
            take("last", last[1], last[2], 1)
        if across is not None:
            take("part", stream["part"], (0, 0), 1)
            take("moved", moved, (0, 0), 1)
        if entering is not None:
            take("next", entering[1], entering[2], 0)
        given = []
        if last is not None:
            given.append("part")
        if across is not None or entering is not None:
            given.append("send")
        if not given:
            return None, None

        def kernel(where_ref, *refs):
            read = dict(zip(names, refs))
            write = dict(zip(given, refs[len(names) :]))

            @pl.when(where_ref[0] == 1)
            def _():
                if "last" in read:
                    total = read["last"][...].astype(F32) + read["came"][...].astype(F32)
                    write["part"][...] = total.astype(BF)
                if "part" in read:
                    total = read["part"][...].astype(F32) + read["moved"][...].astype(F32)
                    write["send"][...] = total.astype(BF)

            if "next" in read:

                @pl.when(where_ref[0] == 0)
                def _():
                    write["send"][...] = read["next"][...]

        results = pl.pallas_call(
            kernel,
            grid_spec=pltpu.PrefetchScalarGridSpec(
                num_scalar_prefetch=1,
                grid=(steps,),
                in_specs=[one[1] for one in inputs],
                out_specs=[
                    pl.BlockSpec(
                        (tile, wide),
                        lambda i, w: (i, 0)
                        if name == "send"
                        else (jnp.where(w[0] == 1, i, 0), 0),
                    )
                    for name in given
                ],
            ),
            out_shape=[jax.ShapeDtypeStruct((rows, wide), BF)] * len(given),
            compiler_params=pltpu.CompilerParams(vmem_limit_bytes=16 * 2**20),
            cost_estimate=pl.CostEstimate(flops=0, bytes_accessed=1, transcendentals=0),
        )(self.inner.astype(jnp.int32)[None], *[one[0] for one in inputs])
        results = dict(zip(given, results))
        return results.get("part"), results.get("send")


def place(shape, mine, other, rows, wide, blocks):
    core = lax.axis_index("core")
    table = jnp.asarray(
        [[list(there) + list(here(k)) for k in range(2)] for there, here in blocks], jnp.int32
    )
    table = jnp.stack([table[:, 0], table[:, 1]])
    table = jnp.where(core == 0, table, table[::-1])
    count = len(blocks)
    table = table.reshape(-1)
    size = table.shape[0] // (2 * count)

    def entry(w, k, j, field):
        return w[(k * count + j) * size + field]

    def source(k, j, w, own):
        j = jnp.where(k == own, j, count - 1 if own == 0 else 0)
        return tuple(entry(w, k, j, field) for field in range(3))

    def kernel(table_ref, mine_ref, other_ref, out_ref):
        @pl.when(pl.program_id(0) == 0)
        def _():
            out_ref[...] = mine_ref[...].astype(F32)

        @pl.when(pl.program_id(0) == 1)
        def _():
            out_ref[...] = other_ref[...].astype(F32)

    return pl.pallas_call(
        kernel,
        grid_spec=pltpu.PrefetchScalarGridSpec(
            num_scalar_prefetch=1,
            grid=(2, count),
            in_specs=[
                pl.BlockSpec((None, rows, wide), lambda k, j, w: source(k, j, w, 0)),
                pl.BlockSpec((None, rows, wide), lambda k, j, w: source(k, j, w, 1)),
            ],
            out_specs=pl.BlockSpec(
                (rows, wide), lambda k, j, w: (entry(w, k, j, 3), entry(w, k, j, 4))
            ),
        ),
        out_shape=jax.ShapeDtypeStruct(shape, F32),
        compiler_params=pltpu.CompilerParams(vmem_limit_bytes=16 * 2**20),
        cost_estimate=pl.CostEstimate(
            flops=0, bytes_accessed=12 * count * rows * wide, transcendentals=0
        ),
    )(table, mine, other)


def body(
    tokens,
    seq_lengths,
    attn_gain,
    w_query,
    w_key,
    w_value,
    w_out,
    mlp_gain,
    w_gate,
    w_up,
    w_down,
    cotangent,
):
    parts = lax.axis_size("group")
    cores = lax.axis_size("core")
    g = lax.axis_index("group")
    c = lax.axis_index("core")
    rows, width = tokens.shape[1:]
    total = rows * parts
    team = parts * cores
    heads = HQ // HK
    scale = HEAD ** (-0.5)
    ff = w_gate.shape[1] // team
    share = w_gate.shape[0]
    qw = HQ * HEAD // team
    kw = HK * HEAD // team
    assert kw == HEAD

    def columns(weight, size, rows=slice(None)):
        return jnp.stack(
            [
                lax.dynamic_slice_in_dim(weight[rows], (k * cores + c) * size, size, 1)
                for k in range(parts)
            ]
        )

    def fetch(blocks):
        return [
            step_to(lax.dynamic_index_in_dim(blocks, g ^ s, 0, keepdims=False), "group", s)
            for s in range(1, parts)
        ]

    def in_order(own, got):
        out = jnp.zeros((parts,) + own.shape, own.dtype)
        for s, block in enumerate([own] + got):
            out = lax.dynamic_update_slice_in_dim(out, block[None], g ^ s, 0)
        return out.reshape((parts * own.shape[0],) + own.shape[1:])

    def own_columns(weight, size):
        return lax.dynamic_slice_in_dim(weight, (g * cores + c) * size, size, 1)

    clock = Clock()
    x_mine = tokens[0]
    extra = 2 * share // width if 2 * share > width else 1
    gains = jnp.concatenate([attn_gain, mlp_gain])
    gains = jnp.pad(gains, (0, 16 * width - gains.shape[0])).reshape(16, width)
    x_got = spread(jnp.concatenate([x_mine, gains], axis=0))
    x_got = x_got.reshape(parts, rows + 16, width)
    gains = x_got[:, rows].reshape(parts, width)[:, : 2 * share]
    gain_one = gains[:, :share].reshape(-1).astype(F32)
    gain_two = gains[:, share:].reshape(-1).astype(F32)
    x_got = x_got[:, :rows].reshape(parts * rows, width)
    qkv_send = jnp.concatenate(
        [columns(w_query, qw), columns(w_key, kw), columns(w_value, kw)], axis=2
    )
    qkv_got = fetch(qkv_send)
    qkv_own = lax.dynamic_index_in_dim(qkv_send, g, 0, keepdims=False)

    paired = lax.axis_size("rest") == 4
    even = lax.axis_index("rest") % 2 == 0
    halves = [slice(0, share // 4 * 3), slice(share // 4 * 3, share)]
    sends = []
    for half in halves:
        gate_send = columns(w_gate, ff, half)
        up_send = columns(w_up, ff, half)
        sends.append([jnp.where(even, gate_send, up_send)] if paired else [gate_send, up_send])
    lengths = [seq_lengths[0]]
    if cores == 2:
        lengths.append(from_core(seq_lengths[0]))
    index = jnp.arange(total, dtype=jnp.int32)
    marks = [positions_of(one, index) for one in lengths]
    half = HEAD // 2
    freq = BASE ** (-(2.0 * jnp.arange(half, dtype=F32)) / HEAD)
    place_all = jnp.concatenate([one[1] for one in marks]).astype(F32)
    angle = place_all[:, None] * jnp.tile(freq, 128 // half)[None, :]
    cosine, sine = jnp.cos(angle), jnp.sin(angle)
    marks_row = jnp.stack([jnp.stack([one[1], one[0]]) for one in marks])
    marks_column = marks_row.transpose(0, 2, 1)
    x_got, qkv_got, sends, cosine, sine, marks_row, marks_column = clock.tick(
        x_got, qkv_got, sends, cosine, sine, marks_row, marks_column
    )

    out_rows = lax.dynamic_slice_in_dim(w_out, c * qw, qw, 0)
    down_rows = lax.dynamic_slice_in_dim(w_down, c * ff, ff, 0)
    first_got = [[fetch(one) for one in sends[0]]]
    second_got = []
    qkv_full = in_order(qkv_own, qkv_got)
    x_all = with_core(x_got)

    def swap(got):
        return step_to(jnp.stack(got[0]), "rest", 1)

    def fill(out, got, row):
        for s in range(1, parts):
            out = lax.dynamic_update_slice(out, got[s - 1][None], (g ^ s, row, 0))
        return out

    def begin(own):
        return lax.dynamic_update_slice_in_dim(
            jnp.zeros((parts, share, ff), BF), own[None], g, 0
        )

    def ordered(first, second):
        if not paired:
            return first, second
        return jnp.where(even, first, second), jnp.where(even, second, first)

    x = x_all.astype(F32)
    inverse_all = lax.rsqrt(jnp.mean(x * x, axis=1, keepdims=True) + EPS)
    normed_one = (x * inverse_all * gain_one).astype(BF)
    qkv = matmul(normed_one, qkv_full)
    attended, kept, logsum = by_group(
        forward_kernel,
        total,
        cores,
        [qkv, cosine, sine, marks_column, marks_row],
        [
            jax.ShapeDtypeStruct((cores * total, qw), BF),
            jax.ShapeDtypeStruct((cores * total, qw + 2 * kw), BF),
            jax.ShapeDtypeStruct((cores * total, 128), F32),
        ],
    )
    x_own = x_mine.astype(F32)
    send = scatter_send(matmul(attended, out_rows))
    send, first_got, kept, attended, logsum = clock.tick(
        send, first_got, kept, attended, logsum
    )

    if paired:
        second_got.append(swap(first_got[0]))
    first_got.append([fetch(clock.now(one)) for one in sends[1]])
    own = [own_columns(w_gate, ff), own_columns(w_up, ff)]
    if paired:
        own = ordered(*own)
    first_full = fill(begin(clock.now(own[0])), first_got[0][0], 0)
    second_full = begin(clock.now(own[1]))
    mid = x_own + scatter_sum(send)
    mid, first_got, first_full, second_full = clock.tick(
        mid, first_got, first_full, second_full
    )

    inverse_two = lax.rsqrt(jnp.mean(mid * mid, axis=1, keepdims=True) + EPS)
    unit_two = mid * inverse_two
    if paired:
        second_got.append(swap(first_got[1]))
    normed_two = spread((unit_two * gain_two).astype(BF))
    cot_all = spread(clock.now(cotangent[0]))
    split = share // 4 * 3
    first_full = fill(first_full, first_got[1][0], split)
    others = second_got if paired else [got[1] for got in first_got]
    second_full = fill(second_full, others[0], 0)
    normed_two, second_got, unit_two, inverse_two, first_full, second_full = clock.tick(
        normed_two, second_got, unit_two, inverse_two, first_full, second_full
    )
    normed_two = with_core(normed_two)
    cot_all = with_core(cot_all)
    others = second_got if paired else [got[1] for got in first_got]
    second_full = fill(second_full, others[1], split)
    first_full = first_full.reshape(share * parts, ff)
    second_full = second_full.reshape(share * parts, ff)
    gate, up = ordered(matmul(normed_two, first_full), matmul(normed_two, second_full))
    sigma = jax.nn.sigmoid(gate)
    active = (gate * sigma * up).astype(BF)
    grad_down = contract_first(active, cot_all).astype(BF)
    on_line = paired and cores == 2
    line = Line(clock, (share, ff))
    outs = {}

    def slot(entering, *values):
        if on_line:
            return line.slot(entering, *values)
        return clock.tick(*values) if values else None

    active, cot_all, grad_down = slot(
        (("down", 0), grad_down, (0, 0)), active, cot_all, grad_down
    )
    grad_active = contract_last(cot_all, down_rows)
    grad_gate_pre = (grad_active * up * sigma * (1.0 + gate * (1.0 - sigma))).astype(BF)
    grad_up_pre = (grad_active * gate * sigma).astype(BF)
    first_pre, second_pre = ordered(grad_gate_pre, grad_up_pre)
    partial = contract_last(first_pre, first_full) + contract_last(second_pre, second_full)
    grad_gate_pre, grad_up_pre, partial = slot(
        (("down", 1), grad_down, (0, 1)), grad_gate_pre, grad_up_pre, partial
    )
    grad_normed_two = scatter_sum(scatter_send(partial))
    grad_gate = contract_first(normed_two, grad_gate_pre).astype(BF)
    grad_gate = clock.tick(grad_gate) if not on_line else grad_gate
    slot((("gate", 0), grad_gate, (0, 0)))
    grad_up = contract_first(normed_two, clock.now(grad_up_pre)).astype(BF)
    grad_up, grad_normed_two = slot((("gate", 1), grad_gate, (1, 0)), grad_up, grad_normed_two)
    grad_y = cotangent[0].astype(F32)
    grad_gain_two = jnp.sum(grad_normed_two * unit_two, axis=0)
    grad_mid = grad_y + norm_back(grad_normed_two, unit_two, inverse_two, gain_two)
    grad_branch = spread(grad_mid.astype(BF))
    grad_mid, grad_gain_two, grad_branch = slot(
        (("gate", 2), grad_gate, (2, 0)), grad_mid, grad_gain_two, grad_branch
    )
    grad_branch = with_core(grad_branch)
    grad_attended = contract_last(grad_branch, out_rows).astype(BF)
    grad_out = contract_first(attended, grad_branch).astype(BF)
    grad_attended, grad_out = slot(
        (("gate", 3), grad_gate, (3, 0)), grad_attended, grad_out
    )

    def both(mine):
        mine = clock.now(mine)
        return mine, from_core(mine)

    (grad_qkv,) = by_group(
        backward_kernel,
        total,
        cores,
        [kept, logsum, grad_attended, cosine, sine, marks_column, marks_row],
        [jax.ShapeDtypeStruct((cores * total, qw + 2 * kw), BF)],
        [pltpu.VMEM((total, qw + 2 * kw), F32)],
    )
    grad_qkv = slot((("up", 0), grad_up, (0, 0)), grad_qkv)
    grad_weights = contract_first(normed_one, grad_qkv).astype(BF)
    send = scatter_send(contract_last(grad_qkv, qkv_full))
    grad_weights, send = slot((("up", 1), grad_up, (1, 0)), grad_weights, send)
    grad_normed_one = scatter_sum(send)
    grad_normed_one = slot((("up", 2), grad_up, (2, 0)), grad_normed_one)
    inverse_one = lax.rsqrt(jnp.mean(x_own * x_own, axis=1, keepdims=True) + EPS)
    unit_one = x_own * inverse_one
    grad_gain_one = jnp.sum(grad_normed_one * unit_one, axis=0)
    grad_x = grad_mid + norm_back(grad_normed_one, unit_one, inverse_one, gain_one)
    each = qw + 2 * kw
    grad_gains = jnp.stack([grad_gain_one, grad_gain_two]).reshape(2, parts, share)
    grad_gains = grad_gains.transpose(1, 0, 2).reshape(parts, 2 * share).astype(BF)
    grad_gains = jnp.pad(grad_gains, ((0, 0), (0, 16 * each - 2 * share)))
    turned = exchange(
        jnp.concatenate(
            [grad_weights.reshape(parts, share, each), grad_gains.reshape(parts, 16, each)],
            axis=1,
        )
    )
    turned, grad_x = slot((("up", 3), grad_up, (3, 0)), turned, grad_x)
    grad_gains = turned[:, share:].reshape(parts, 16 * each)[:, : 2 * share]
    grad_gains = jnp.sum(grad_gains.reshape(parts, 2, share).astype(F32), axis=0)
    turned = turned[:, :share]
    turned_q = turned[:, :, :qw].transpose(1, 0, 2).reshape(share, parts * qw)
    turned_kv = turned[:, :, qw:].transpose(1, 0, 2).reshape(share, parts * 2 * kw)
    if on_line:
        turned_kv = jnp.concatenate(
            [
                turned_kv,
                jnp.pad(
                    grad_gains.astype(BF), ((0, share - 2), (0, ff - parts * 2 * kw - share))
                ),
            ],
            axis=1,
        )

        def turn(name):
            return exchange(line.stack(name, parts))

        def place_columns(turned):
            return place(
                (share, ff * team),
                *both(turned),
                share,
                ff,
                [((j, 0, 0), lambda k, j=j: (0, j * 2 + k)) for j in range(parts)],
            )

        gate_turned = turn("gate")
        grad_out = jnp.concatenate([grad_out[:, :ff], grad_out[:, ff:]], axis=0)
        turned_q, turned_kv, grad_out = slot(
            (("down", 2), grad_down, (1, 0)), turned_q, turned_kv, grad_out
        )
        result = matmul(clock.now(active), down_rows)
        gate_turned, result = slot(
            (("down", 3), grad_down, (1, 1)), gate_turned, result
        )
        outs["gate"] = place_columns(gate_turned)
        outs = slot((("heads", 0), turned_q, (0, 0)), outs)
        up_turned = turn("up")
        slot((("heads", 1), turned_kv, (0, 0)))
        result = scatter_send(clock.now(result))
        up_turned, result = slot((("rows", 0), grad_out, (0, 0)), up_turned, result)
        outs["up"] = place_columns(up_turned)
        result = mid + scatter_sum(result)
        outs, result = slot(None, outs, result)
        outs["down"] = place(
            (ff * 2, width),
            *both(line.stack("down", 4)),
            share,
            ff,
            [
                ((a * 2 + b, 0, 0), lambda k, a=a, b=b: (k * 2 + a, b))
                for a in range(2)
                for b in range(2)
            ],
        )
        outs = slot(None, outs)
        mine, other = both(line.stack("heads", 2))
        grad_gains = sum(
            one[1, :2, parts * 2 * kw : parts * 2 * kw + share].astype(F32) for one in (mine, other)
        )
        outs["query"] = place(
            (share, qw * team),
            mine,
            other,
            share,
            qw,
            [((0, 0, j), lambda k, j=j: (0, j * 2 + k)) for j in range(parts)],
        )
        narrow = [
            one[1, :, : parts * 2 * kw].reshape(share, parts, 2 * kw) for one in (mine, other)
        ]
        narrow = jnp.stack(
            [jnp.where(c == 0, *narrow), jnp.where(c == 0, *narrow[::-1])], axis=2
        ).astype(F32)
        outs["key"] = narrow[..., :kw].reshape(share, team * kw)
        outs["value"] = narrow[..., kw:].reshape(share, team * kw)
        outs = slot(None, outs)
        outs["out"] = place(
            (qw * 2, width),
            *both(line.stack("rows", 1)),
            qw,
            ff,
            [((0, b, 0), lambda k, b=b: (k, b)) for b in range(2)],
        )
    else:
        result = mid + scatter_sum(scatter_send(matmul(active, down_rows)))

        def whole(value):
            value = lax.psum(value, "rest")[None]
            if cores == 2:
                other = from_core(value)
                value = jnp.concatenate(
                    [jnp.where(c == 0, value, other), jnp.where(c == 0, other, value)]
                )
            return value.astype(F32)

        def beside(value):
            return value.transpose(2, 1, 0, 3).reshape(share, -1)

        grad_gains = lax.psum(grad_gains, ("rest", "core"))
        outs["down"] = whole(grad_down).reshape(cores * ff, width)
        outs["out"] = whole(grad_out).reshape(cores * qw, width)
        for name, grad in (("gate", grad_gate), ("up", grad_up)):
            outs[name] = beside(whole(exchange(grad.reshape(parts, share, ff))))
        turned = whole(turned)
        outs["query"] = beside(turned[..., :qw])
        outs["key"] = beside(turned[..., qw : qw + kw])
        outs["value"] = beside(turned[..., qw + kw :])
    return (
        result.astype(BF)[None],
        grad_x.astype(BF)[None],
        grad_gains[0],
        outs["query"],
        outs["key"],
        outs["value"],
        outs["out"],
        grad_gains[1],
        outs["gate"],
        outs["up"],
        outs["down"],
    )


def solution(mesh):
    parts, replicas = mesh.devices.shape
    cores = 2 if HK % (2 * parts) == 0 and replicas % 2 == 0 else 1
    split = Mesh(
        mesh.devices.reshape(parts, replicas // cores, cores), ("group", "rest", "core")
    )
    replica = ("rest", "core")
    weights = (P("group"),) + (P("group", None),) * 4 + (P("group"),) + (P("group", None),) * 3
    split_tokens = P(replica, "group", None)
    return jax.shard_map(
        body,
        mesh=split,
        in_specs=(split_tokens, P(replica, None)) + weights + (split_tokens,),
        out_specs=(split_tokens, split_tokens) + weights,
        check_vma=False,
    )
```

```python
import jax
import jax.numpy as jnp
from jax import lax
from jax.experimental import pallas as pl
from jax.experimental.pallas import tpu as pltpu
from jax.sharding import Mesh
from jax.sharding import PartitionSpec as P

HQ = 32
HK = 8
HEAD = 64

EPS = 1e-05
BASE = 500000.0
MASKED = -1e30

BF = jnp.bfloat16
F32 = jnp.float32


def positions_of(lengths, index):
    ends = jnp.cumsum(lengths)
    starts = ends - lengths
    segment = jnp.sum((index[:, None] >= ends[None, :-1]).astype(jnp.int32), axis=1)
    member = segment[:, None] == jnp.arange(lengths.shape[0], dtype=jnp.int32)[None, :]
    start = jnp.sum(jnp.where(member, starts[None, :], 0), axis=1)
    place = jnp.where(segment == 0, index, lengths[0] + index - start)
    return (segment, place)


def matmul(left, right):
    return jnp.dot(left, right, preferred_element_type=F32)


def contract_last(left, right):
    return lax.dot_general(left, right, (((1,), (1,)), ((), ())), preferred_element_type=F32)


def contract_first(left, right):
    return lax.dot_general(left, right, (((0,), (0,)), ((), ())), preferred_element_type=F32)


def norm_back(grad_normed, unit, inverse, gain):
    scaled = grad_normed * gain
    return inverse * (scaled - unit * jnp.mean(scaled * unit, axis=1, keepdims=True))


def after(value, *others):
    return lax.optimization_barrier((value,) + others)[0]


def after(value, *others):
    return lax.optimization_barrier((value,) + others)[0]


def step_to(value, axis, step):
    size = lax.axis_size(axis)
    return lax.ppermute(value, axis, [(i, i ^ step) for i in range(size)])


def exchange(blocks):
    return lax.all_to_all(blocks, "group", 0, 0, tiled=True)


def spread(mine):
    parts = lax.axis_size("group")
    blocks = exchange(jnp.broadcast_to(mine[None], (parts,) + mine.shape))
    return blocks.reshape((parts * mine.shape[0],) + mine.shape[1:])


def from_core(value):
    return step_to(value, "core", 1)


def with_core(got):
    if lax.axis_size("core") == 1:
        return got
    return jnp.concatenate([got, from_core(got)], axis=0)


def scatter_send(partial):
    parts = lax.axis_size("group")
    if lax.axis_size("core") == 2:
        half = partial.shape[0] // 2
        partial = partial[:half] + from_core(partial[half:].astype(BF)).astype(F32)
    rows = partial.shape[0] // parts
    return partial.astype(BF).reshape((parts, rows) + partial.shape[1:])


def scatter_sum(blocks):
    return jnp.sum(exchange(blocks).astype(F32), axis=0)


def rotated(value, cosine, sine, back):
    wide = value.shape[1]
    half = HEAD // 2
    lane = lax.broadcasted_iota(jnp.int32, value.shape, 1)
    low = lane % HEAD < half
    other = jnp.where(
        low, pltpu.roll(value, wide - half, 1), pltpu.roll(value, half, 1)
    )
    sign = jnp.where(low, -1.0, 1.0)
    if back:
        sign = -sign
    return value * cosine + other * sign * sine


def visible(place_query, segment_query, place_key, segment_key):
    same = (segment_key == 0) | (segment_key == segment_query)
    return same & (place_key <= place_query)


def forward_kernel(qkv_ref, cos_ref, sin_ref, column_ref, row_ref, o_ref, kept_ref, lse_ref):
    heads = HQ // HK
    wide = heads * HEAD
    scale = HEAD ** (-0.5)
    cosine, sine = cos_ref[...], sin_ref[...]
    tiles = wide // cosine.shape[1]
    query = rotated(
        qkv_ref[:, :wide],
        jnp.concatenate([cosine] * tiles, axis=1),
        jnp.concatenate([sine] * tiles, axis=1),
        False,
    )
    query = query.astype(BF)
    pair = qkv_ref[:, wide:]
    lane = lax.broadcasted_iota(jnp.int32, pair.shape, 1)
    pair = jnp.where(lane < HEAD, rotated(pair, cosine, sine, False), pair).astype(BF)
    kept_ref[:, :wide] = query
    kept_ref[:, wide:] = pair
    key, value = pair[:, :HEAD], pair[:, HEAD:]
    allowed = visible(column_ref[:, 0:1], column_ref[:, 1:2], row_ref[0:1, :], row_ref[1:2, :])
    found = []
    for h in range(heads):
        one = query[:, h * HEAD : (h + 1) * HEAD]
        scores = jnp.where(allowed, contract_last(one, key) * scale, MASKED)
        top = jnp.max(scores, axis=1, keepdims=True)
        expo = jnp.exp(scores - top)
        denom = jnp.sum(expo, axis=1, keepdims=True)
        probs = (expo / denom).astype(BF)
        o_ref[:, h * HEAD : (h + 1) * HEAD] = matmul(probs, value).astype(BF)
        found.append(top + jnp.log(denom))
    place = lax.broadcasted_iota(jnp.int32, lse_ref.shape, 1)
    total = jnp.zeros(lse_ref.shape, F32)
    for h in range(heads):
        total = jnp.where(place == h, found[h], total)
    lse_ref[...] = total


def backward_kernel(
    kept_ref, lse_ref, grad_ref, cos_ref, sin_ref, column_ref, row_ref, out_ref, hold_ref
):
    heads = HQ // HK
    wide = heads * HEAD
    scale = HEAD ** (-0.5)
    key = kept_ref[:, wide : wide + HEAD]
    value = kept_ref[:, wide + HEAD :]
    allowed = visible(column_ref[:, 0:1], column_ref[:, 1:2], row_ref[0:1, :], row_ref[1:2, :])
    total = key.shape[0]
    grad_k = jnp.zeros((total, HEAD), F32)
    grad_v = jnp.zeros((total, HEAD), F32)
    for h in range(heads):
        one = kept_ref[:, h * HEAD : (h + 1) * HEAD]
        grad = grad_ref[:, h * HEAD : (h + 1) * HEAD]
        scores = jnp.where(allowed, contract_last(one, key) * scale, MASKED)
        probs = jnp.exp(scores - lse_ref[:, h : h + 1])
        grad_p = contract_last(grad, value)
        grad_s = probs * (grad_p - jnp.sum(probs * grad_p, axis=1, keepdims=True))
        grad_s = grad_s.astype(BF)
        hold_ref[:, h * HEAD : (h + 1) * HEAD] = matmul(grad_s, key) * scale
        grad_k = grad_k + contract_first(grad_s, one)
        grad_v = grad_v + contract_first(probs.astype(BF), grad)
    hold_ref[:, wide : wide + HEAD] = grad_k * scale
    hold_ref[:, wide + HEAD :] = grad_v
    cosine, sine = cos_ref[...], sin_ref[...]
    tiles = wide // cosine.shape[1]
    out_ref[:, :wide] = rotated(
        hold_ref[:, :wide],
        jnp.concatenate([cosine] * tiles, axis=1),
        jnp.concatenate([sine] * tiles, axis=1),
        True,
    ).astype(BF)
    pair = hold_ref[:, wide:]
    lane = lax.broadcasted_iota(jnp.int32, pair.shape, 1)
    pair = jnp.where(lane < HEAD, rotated(pair, cosine, sine, True), pair)
    out_ref[:, wide:] = pair.astype(BF)


def by_group(kernel, total, groups, inputs, outputs, scratch=()):
    def spec(shape):
        if len(shape) == 3:
            return pl.BlockSpec((None,) + shape[1:], lambda i: (i, 0, 0))
        return pl.BlockSpec((total, shape[1]), lambda i: (i, 0))

    return pl.pallas_call(
        kernel,
        grid=(groups,),
        in_specs=[spec(one.shape) for one in inputs],
        out_specs=[spec(one.shape) for one in outputs],
        out_shape=list(outputs),
        scratch_shapes=list(scratch),
        compiler_params=pltpu.CompilerParams(vmem_limit_bytes=40 * 2**20),
        cost_estimate=pl.CostEstimate(flops=0, bytes_accessed=1, transcendentals=0),
    )(*inputs)


class Clock:
    def __init__(self):
        self.token = jnp.zeros((8, 128), F32)

    def tick(self, *values):
        flat, tree = jax.tree.flatten(values)
        out = lax.optimization_barrier((self.token, *flat))
        self.token = out[0]
        values = jax.tree.unflatten(tree, out[1:])
        return values[0] if len(values) == 1 else values

    def now(self, value):
        return after(value, self.token)


class Line:
    def __init__(self, clock, shape):
        self.clock = clock
        self.shape = shape
        place = lax.axis_index("rest")
        self.inner = (place == 1) | (place == 2)
        self.sums = {}
        self.flight = {}

    def piece(self, array, block):
        rows, wide = self.shape
        if array.ndim == 3:
            return array[block[0]]
        row, column = block
        return array[row * rows : (row + 1) * rows, column * wide : (column + 1) * wide]

    def slot(self, entering, *values):
        last = self.flight
        came, moved, values = self.clock.tick(last.get("came"), last.get("moved"), values)
        if entering is not None:
            name, array, block = entering
            entering = (name, self.clock.now(array), block)
        part, send = self.combine(last, came, moved, entering)
        across = last["enter"][0] if part is not None else None
        flight = {"enter": entering, "across": across, "part": part}
        if last.get("across"):
            flight["out"] = (last["across"], send)
        if part is not None:
            flight["moved"] = lax.ppermute(part, "rest", [(1, 2), (2, 1)])
        if send is not None:
            flight["came"] = lax.ppermute(send, "rest", [(0, 1), (1, 0), (2, 3), (3, 2)])
        if last.get("out"):
            name, full = last["out"]
            self.sums[name] = (full, came)
        self.flight = flight
        return values[0] if len(values) == 1 else values

    def stack(self, name, count):
        rows, wide = self.shape
        steps = 2
        tile = rows // steps
        pairs = [self.sums[name, k] for k in range(count)]

        def spec(k, used):
            def at(j, i, w):
                here = jnp.where(j == k, i, jnp.where(j < k, 0, steps - 1))
                return (jnp.where(w[0] == used, here, 0), 0)

            return pl.BlockSpec((tile, wide), at)

        def kernel(where_ref, *refs):
            for k in range(count):
                for used in range(2):

                    @pl.when((pl.program_id(0) == k) & (where_ref[0] == used))
                    def _(k=k, used=used):
                        refs[-1][...] = refs[2 * k + 1 - used][...]

        return pl.pallas_call(
            kernel,
            grid_spec=pltpu.PrefetchScalarGridSpec(
                num_scalar_prefetch=1,
                grid=(count, steps),
                in_specs=[spec(k, used) for k in range(count) for used in (1, 0)],
                out_specs=pl.BlockSpec((None, tile, wide), lambda j, i, w: (j, i, 0)),
            ),
            out_shape=jax.ShapeDtypeStruct((count, rows, wide), BF),
            compiler_params=pltpu.CompilerParams(vmem_limit_bytes=16 * 2**20),
            cost_estimate=pl.CostEstimate(flops=0, bytes_accessed=1, transcendentals=0),
        )(self.inner.astype(jnp.int32)[None], *[one for pair in pairs for one in pair])

    def combine(self, stream, came, moved, entering):
        rows, wide = self.shape
        steps = 2
        tile = rows // steps
        last, across = stream.get("enter"), stream.get("across")

        def spec(block, used):
            def at(i, w):
                here = jnp.where(w[0] == used, i, 0)
                return block[:-2] + (block[-2] * steps + here, block[-1])

            return pl.BlockSpec((None,) * (len(block) - 2) + (tile, wide), at)

        inputs, names = [], []

        def take(name, array, block, used):
            inputs.append((array, spec(block, used)))
            names.append(name)

        if last is not None:
            take("came", came, (0, 0), 1)
            take("last", last[1], last[2], 1)
        if across is not None:
            take("part", stream["part"], (0, 0), 1)
            take("moved", moved, (0, 0), 1)
        if entering is not None:
            take("next", entering[1], entering[2], 0)
        given = []
        if last is not None:
            given.append("part")
        if across is not None or entering is not None:
            given.append("send")
        if not given:
            return None, None

        def kernel(where_ref, *refs):
            read = dict(zip(names, refs))
            write = dict(zip(given, refs[len(names) :]))

            @pl.when(where_ref[0] == 1)
            def _():
                if "last" in read:
                    total = read["last"][...].astype(F32) + read["came"][...].astype(F32)
                    write["part"][...] = total.astype(BF)
                if "part" in read:
                    total = read["part"][...].astype(F32) + read["moved"][...].astype(F32)
                    write["send"][...] = total.astype(BF)

            if "next" in read:

                @pl.when(where_ref[0] == 0)
                def _():
                    write["send"][...] = read["next"][...]

        results = pl.pallas_call(
            kernel,
            grid_spec=pltpu.PrefetchScalarGridSpec(
                num_scalar_prefetch=1,
                grid=(steps,),
                in_specs=[one[1] for one in inputs],
                out_specs=[
                    pl.BlockSpec(
                        (tile, wide),
                        lambda i, w: (i, 0)
                        if name == "send"
                        else (jnp.where(w[0] == 1, i, 0), 0),
                    )
                    for name in given
                ],
            ),
            out_shape=[jax.ShapeDtypeStruct((rows, wide), BF)] * len(given),
            compiler_params=pltpu.CompilerParams(vmem_limit_bytes=16 * 2**20),
            cost_estimate=pl.CostEstimate(flops=0, bytes_accessed=1, transcendentals=0),
        )(self.inner.astype(jnp.int32)[None], *[one[0] for one in inputs])
        results = dict(zip(given, results))
        return results.get("part"), results.get("send")


def place(shape, mine, other, rows, wide, blocks):
    core = lax.axis_index("core")
    table = jnp.asarray(
        [[list(there) + list(here(k)) for k in range(2)] for there, here in blocks], jnp.int32
    )
    table = jnp.stack([table[:, 0], table[:, 1]])
    table = jnp.where(core == 0, table, table[::-1])
    count = len(blocks)
    table = table.reshape(-1)
    size = table.shape[0] // (2 * count)

    def entry(w, k, j, field):
        return w[(k * count + j) * size + field]

    def source(k, j, w, own):
        j = jnp.where(k == own, j, count - 1 if own == 0 else 0)
        return tuple(entry(w, k, j, field) for field in range(3))

    def kernel(table_ref, mine_ref, other_ref, out_ref):
        @pl.when(pl.program_id(0) == 0)
        def _():
            out_ref[...] = mine_ref[...].astype(F32)

        @pl.when(pl.program_id(0) == 1)
        def _():
            out_ref[...] = other_ref[...].astype(F32)

    return pl.pallas_call(
        kernel,
        grid_spec=pltpu.PrefetchScalarGridSpec(
            num_scalar_prefetch=1,
            grid=(2, count),
            in_specs=[
                pl.BlockSpec((None, rows, wide), lambda k, j, w: source(k, j, w, 0)),
                pl.BlockSpec((None, rows, wide), lambda k, j, w: source(k, j, w, 1)),
            ],
            out_specs=pl.BlockSpec(
                (rows, wide), lambda k, j, w: (entry(w, k, j, 3), entry(w, k, j, 4))
            ),
        ),
        out_shape=jax.ShapeDtypeStruct(shape, F32),
        compiler_params=pltpu.CompilerParams(vmem_limit_bytes=16 * 2**20),
        cost_estimate=pl.CostEstimate(
            flops=0, bytes_accessed=12 * count * rows * wide, transcendentals=0
        ),
    )(table, mine, other)


def body(
    tokens,
    seq_lengths,
    attn_gain,
    w_query,
    w_key,
    w_value,
    w_out,
    mlp_gain,
    w_gate,
    w_up,
    w_down,
    cotangent,
):
    parts = lax.axis_size("group")
    cores = lax.axis_size("core")
    g = lax.axis_index("group")
    c = lax.axis_index("core")
    rows, width = tokens.shape[1:]
    total = rows * parts
    team = parts * cores
    heads = HQ // HK
    scale = HEAD ** (-0.5)
    ff = w_gate.shape[1] // team
    share = w_gate.shape[0]
    qw = HQ * HEAD // team
    kw = HK * HEAD // team
    assert kw == HEAD

    def columns(weight, size, rows=slice(None)):
        return jnp.stack(
            [
                lax.dynamic_slice_in_dim(weight[rows], (k * cores + c) * size, size, 1)
                for k in range(parts)
            ]
        )

    def fetch(blocks):
        return [
            step_to(lax.dynamic_index_in_dim(blocks, g ^ s, 0, keepdims=False), "group", s)
            for s in range(1, parts)
        ]

    def in_order(own, got):
        out = jnp.zeros((parts,) + own.shape, own.dtype)
        for s, block in enumerate([own] + got):
            out = lax.dynamic_update_slice_in_dim(out, block[None], g ^ s, 0)
        return out.reshape((parts * own.shape[0],) + own.shape[1:])

    def own_columns(weight, size):
        return lax.dynamic_slice_in_dim(weight, (g * cores + c) * size, size, 1)

    clock = Clock()
    x_mine = tokens[0]
    extra = 2 * share // width if 2 * share > width else 1
    gains = jnp.concatenate([attn_gain, mlp_gain])
    gains = jnp.pad(gains, (0, 16 * width - gains.shape[0])).reshape(16, width)
    x_got = spread(jnp.concatenate([x_mine, gains], axis=0))
    x_got = x_got.reshape(parts, rows + 16, width)
    gains = x_got[:, rows].reshape(parts, width)[:, : 2 * share]
    gain_one = gains[:, :share].reshape(-1).astype(F32)
    gain_two = gains[:, share:].reshape(-1).astype(F32)
    x_got = x_got[:, :rows].reshape(parts * rows, width)
    qkv_send = jnp.concatenate(
        [columns(w_query, qw), columns(w_key, kw), columns(w_value, kw)], axis=2
    )
    qkv_got = fetch(qkv_send)
    qkv_own = lax.dynamic_index_in_dim(qkv_send, g, 0, keepdims=False)

    paired = lax.axis_size("rest") == 4
    even = lax.axis_index("rest") % 2 == 0
    halves = [slice(0, share // 4 * 3), slice(share // 4 * 3, share)]
    sends = []
    for half in halves:
        gate_send = columns(w_gate, ff, half)
        up_send = columns(w_up, ff, half)
        sends.append([jnp.where(even, gate_send, up_send)] if paired else [gate_send, up_send])
    lengths = [seq_lengths[0]]
    if cores == 2:
        lengths.append(from_core(seq_lengths[0]))
    index = jnp.arange(total, dtype=jnp.int32)
    marks = [positions_of(one, index) for one in lengths]
    half = HEAD // 2
    freq = BASE ** (-(2.0 * jnp.arange(half, dtype=F32)) / HEAD)
    place_all = jnp.concatenate([one[1] for one in marks]).astype(F32)
    angle = place_all[:, None] * jnp.tile(freq, 128 // half)[None, :]
    cosine, sine = jnp.cos(angle), jnp.sin(angle)
    marks_row = jnp.stack([jnp.stack([one[1], one[0]]) for one in marks])
    marks_column = marks_row.transpose(0, 2, 1)
    x_got, qkv_got, sends, cosine, sine, marks_row, marks_column = clock.tick(
        x_got, qkv_got, sends, cosine, sine, marks_row, marks_column
    )

    out_rows = lax.dynamic_slice_in_dim(w_out, c * qw, qw, 0)
    down_rows = lax.dynamic_slice_in_dim(w_down, c * ff, ff, 0)
    first_got = [[fetch(one) for one in sends[0]]]
    second_got = []
    qkv_full = in_order(qkv_own, qkv_got)
    x_all = with_core(x_got)

    def swap(got):
        return step_to(jnp.stack(got[0]), "rest", 1)

    def fill(out, got, row):
        for s in range(1, parts):
            out = lax.dynamic_update_slice(out, got[s - 1][None], (g ^ s, row, 0))
        return out

    def begin(own):
        return lax.dynamic_update_slice_in_dim(
            jnp.zeros((parts, share, ff), BF), own[None], g, 0
        )

    def ordered(first, second):
        if not paired:
            return first, second
        return jnp.where(even, first, second), jnp.where(even, second, first)

    x = x_all.astype(F32)
    inverse_all = lax.rsqrt(jnp.mean(x * x, axis=1, keepdims=True) + EPS)
    normed_one = (x * inverse_all * gain_one).astype(BF)
    qkv = matmul(normed_one, qkv_full)
    attended, kept, logsum = by_group(
        forward_kernel,
        total,
        cores,
        [qkv, cosine, sine, marks_column, marks_row],
        [
            jax.ShapeDtypeStruct((cores * total, qw), BF),
            jax.ShapeDtypeStruct((cores * total, qw + 2 * kw), BF),
            jax.ShapeDtypeStruct((cores * total, 128), F32),
        ],
    )
    x_own = x_mine.astype(F32)
    send = scatter_send(matmul(attended, out_rows))
    send, first_got, kept, attended, logsum = clock.tick(
        send, first_got, kept, attended, logsum
    )

    if paired:
        second_got.append(swap(first_got[0]))
    first_got.append([fetch(clock.now(one)) for one in sends[1]])
    own = [own_columns(w_gate, ff), own_columns(w_up, ff)]
    if paired:
        own = ordered(*own)
    first_full = fill(begin(clock.now(own[0])), first_got[0][0], 0)
    second_full = begin(clock.now(own[1]))
    mid = x_own + scatter_sum(send)
    mid, first_got, first_full, second_full = clock.tick(
        mid, first_got, first_full, second_full
    )

    inverse_two = lax.rsqrt(jnp.mean(mid * mid, axis=1, keepdims=True) + EPS)
    unit_two = mid * inverse_two
    if paired:
        second_got.append(swap(first_got[1]))
    normed_two = spread((unit_two * gain_two).astype(BF))
    cot_all = spread(clock.now(cotangent[0]))
    split = share // 4 * 3
    first_full = fill(first_full, first_got[1][0], split)
    others = second_got if paired else [got[1] for got in first_got]
    second_full = fill(second_full, others[0], 0)
    normed_two, second_got, unit_two, inverse_two, first_full, second_full = clock.tick(
        normed_two, second_got, unit_two, inverse_two, first_full, second_full
    )
    normed_two = with_core(normed_two)
    cot_all = with_core(cot_all)
    others = second_got if paired else [got[1] for got in first_got]
    second_full = fill(second_full, others[1], split)
    first_full = first_full.reshape(share * parts, ff)
    second_full = second_full.reshape(share * parts, ff)
    gate, up = ordered(matmul(normed_two, first_full), matmul(normed_two, second_full))
    sigma = jax.nn.sigmoid(gate)
    active = (gate * sigma * up).astype(BF)
    grad_down = contract_first(active, cot_all).astype(BF)
    on_line = paired and cores == 2
    line = Line(clock, (share, ff))
    outs = {}

    def slot(entering, *values):
        if on_line:
            return line.slot(entering, *values)
        return clock.tick(*values) if values else None

    active, cot_all, grad_down = slot(
        (("down", 0), grad_down, (0, 0)), active, cot_all, grad_down
    )
    grad_active = contract_last(cot_all, down_rows)
    grad_gate_pre = (grad_active * up * sigma * (1.0 + gate * (1.0 - sigma))).astype(BF)
    grad_up_pre = (grad_active * gate * sigma).astype(BF)
    first_pre, second_pre = ordered(grad_gate_pre, grad_up_pre)
    partial = contract_last(first_pre, first_full) + contract_last(second_pre, second_full)
    grad_gate_pre, grad_up_pre, partial = slot(
        (("down", 1), grad_down, (0, 1)), grad_gate_pre, grad_up_pre, partial
    )
    grad_normed_two = scatter_sum(scatter_send(partial))
    grad_gate = contract_first(normed_two, grad_gate_pre).astype(BF)
    grad_gate = clock.tick(grad_gate) if not on_line else grad_gate
    slot((("gate", 0), grad_gate, (0, 0)))
    grad_up = contract_first(normed_two, clock.now(grad_up_pre)).astype(BF)
    grad_up, grad_normed_two = slot((("gate", 1), grad_gate, (1, 0)), grad_up, grad_normed_two)
    grad_y = cotangent[0].astype(F32)
    grad_gain_two = jnp.sum(grad_normed_two * unit_two, axis=0)
    grad_mid = grad_y + norm_back(grad_normed_two, unit_two, inverse_two, gain_two)
    grad_branch = spread(grad_mid.astype(BF))
    grad_mid, grad_gain_two, grad_branch = slot(
        (("gate", 2), grad_gate, (2, 0)), grad_mid, grad_gain_two, grad_branch
    )
    grad_branch = with_core(grad_branch)
    grad_attended = contract_last(grad_branch, out_rows).astype(BF)
    grad_out = contract_first(attended, grad_branch).astype(BF)
    grad_attended, grad_out = slot(
        (("gate", 3), grad_gate, (3, 0)), grad_attended, grad_out
    )

    def both(mine):
        mine = clock.now(mine)
        return mine, from_core(mine)

    (grad_qkv,) = by_group(
        backward_kernel,
        total,
        cores,
        [kept, logsum, grad_attended, cosine, sine, marks_column, marks_row],
        [jax.ShapeDtypeStruct((cores * total, qw + 2 * kw), BF)],
        [pltpu.VMEM((total, qw + 2 * kw), F32)],
    )
    grad_qkv = slot((("up", 0), grad_up, (0, 0)), grad_qkv)
    grad_weights = contract_first(normed_one, grad_qkv).astype(BF)
    send = scatter_send(contract_last(grad_qkv, qkv_full))
    grad_weights, send = slot((("up", 1), grad_up, (1, 0)), grad_weights, send)
    grad_normed_one = scatter_sum(send)
    grad_normed_one = slot((("up", 2), grad_up, (2, 0)), grad_normed_one)
    inverse_one = lax.rsqrt(jnp.mean(x_own * x_own, axis=1, keepdims=True) + EPS)
    unit_one = x_own * inverse_one
    grad_gain_one = jnp.sum(grad_normed_one * unit_one, axis=0)
    grad_x = grad_mid + norm_back(grad_normed_one, unit_one, inverse_one, gain_one)
    each = qw + 2 * kw
    grad_gains = jnp.stack([grad_gain_one, grad_gain_two]).reshape(2, parts, share)
    grad_gains = grad_gains.transpose(1, 0, 2).reshape(parts, 2 * share).astype(BF)
    grad_gains = jnp.pad(grad_gains, ((0, 0), (0, 16 * each - 2 * share)))
    turned = exchange(
        jnp.concatenate(
            [grad_weights.reshape(parts, share, each), grad_gains.reshape(parts, 16, each)],
            axis=1,
        )
    )
    turned, grad_x = slot((("up", 3), grad_up, (3, 0)), turned, grad_x)
    grad_gains = turned[:, share:].reshape(parts, 16 * each)[:, : 2 * share]
    grad_gains = jnp.sum(grad_gains.reshape(parts, 2, share).astype(F32), axis=0)
    turned = turned[:, :share]
    turned_q = turned[:, :, :qw].transpose(1, 0, 2).reshape(share, parts * qw)
    turned_kv = turned[:, :, qw:].transpose(1, 0, 2).reshape(share, parts * 2 * kw)
    if on_line:
        turned_kv = jnp.concatenate(
            [
                turned_kv,
                jnp.pad(
                    grad_gains.astype(BF), ((0, share - 2), (0, ff - parts * 2 * kw - share))
                ),
            ],
            axis=1,
        )

        def turn(name):
            return exchange(line.stack(name, parts))

        def place_columns(turned):
            return place(
                (share, ff * team),
                *both(turned),
                share,
                ff,
                [((j, 0, 0), lambda k, j=j: (0, j * 2 + k)) for j in range(parts)],
            )

        gate_turned = turn("gate")
        grad_out = jnp.concatenate([grad_out[:, :ff], grad_out[:, ff:]], axis=0)
        turned_q, turned_kv, grad_out = slot(
            (("down", 2), grad_down, (1, 0)), turned_q, turned_kv, grad_out
        )
        result = matmul(clock.now(active), down_rows)
        gate_turned, result = slot(
            (("down", 3), grad_down, (1, 1)), gate_turned, result
        )
        outs["gate"] = place_columns(gate_turned)
        outs = slot((("heads", 0), turned_q, (0, 0)), outs)
        up_turned = turn("up")
        slot((("heads", 1), turned_kv, (0, 0)))
        result = scatter_send(clock.now(result))
        up_turned, result = slot((("rows", 0), grad_out, (0, 0)), up_turned, result)
        outs["up"] = place_columns(up_turned)
        result = mid + scatter_sum(result)
        outs, result = slot(None, outs, result)
        outs["down"] = place(
            (ff * 2, width),
            *both(line.stack("down", 4)),
            share,
            ff,
            [
                ((a * 2 + b, 0, 0), lambda k, a=a, b=b: (k * 2 + a, b))
                for a in range(2)
                for b in range(2)
            ],
        )
        outs = slot(None, outs)
        mine, other = both(line.stack("heads", 2))
        grad_gains = sum(
            one[1, :2, parts * 2 * kw : parts * 2 * kw + share].astype(F32) for one in (mine, other)
        )
        outs["query"] = place(
            (share, qw * team),
            mine,
            other,
            share,
            qw,
            [((0, 0, j), lambda k, j=j: (0, j * 2 + k)) for j in range(parts)],
        )
        narrow = [
            one[1, :, : parts * 2 * kw].reshape(share, parts, 2 * kw) for one in (mine, other)
        ]
        narrow = jnp.stack(
            [jnp.where(c == 0, *narrow), jnp.where(c == 0, *narrow[::-1])], axis=2
        ).astype(F32)
        outs["key"] = narrow[..., :kw].reshape(share, team * kw)
        outs["value"] = narrow[..., kw:].reshape(share, team * kw)
        outs = slot(None, outs)
        outs["out"] = place(
            (qw * 2, width),
            *both(line.stack("rows", 1)),
            qw,
            ff,
            [((0, b, 0), lambda k, b=b: (k, b)) for b in range(2)],
        )
    else:
        result = mid + scatter_sum(scatter_send(matmul(active, down_rows)))

        def whole(value):
            value = lax.psum(value, "rest")[None]
            if cores == 2:
                other = from_core(value)
                value = jnp.concatenate(
                    [jnp.where(c == 0, value, other), jnp.where(c == 0, other, value)]
                )
            return value.astype(F32)

        def beside(value):
            return value.transpose(2, 1, 0, 3).reshape(share, -1)

        grad_gains = lax.psum(grad_gains, ("rest", "core"))
        outs["down"] = whole(grad_down).reshape(cores * ff, width)
        outs["out"] = whole(grad_out).reshape(cores * qw, width)
        for name, grad in (("gate", grad_gate), ("up", grad_up)):
            outs[name] = beside(whole(exchange(grad.reshape(parts, share, ff))))
        turned = whole(turned)
        outs["query"] = beside(turned[..., :qw])
        outs["key"] = beside(turned[..., qw : qw + kw])
        outs["value"] = beside(turned[..., qw + kw :])
    return (
        result.astype(BF)[None],
        grad_x.astype(BF)[None],
        grad_gains[0],
        outs["query"],
        outs["key"],
        outs["value"],
        outs["out"],
        grad_gains[1],
        outs["gate"],
        outs["up"],
        outs["down"],
    )


def solution(mesh):
    parts, replicas = mesh.devices.shape
    cores = 2 if HK % (2 * parts) == 0 and replicas % 2 == 0 else 1
    split = Mesh(
        mesh.devices.reshape(parts, replicas // cores, cores), ("group", "rest", "core")
    )
    replica = ("rest", "core")
    weights = (P("group"),) + (P("group", None),) * 4 + (P("group"),) + (P("group", None),) * 3
    split_tokens = P(replica, "group", None)
    return jax.shard_map(
        body,
        mesh=split,
        in_specs=(split_tokens, P(replica, None)) + weights + (split_tokens,),
        out_specs=(split_tokens, split_tokens) + weights,
        check_vma=False,
    )
```

```python
import jax
import jax.numpy as jnp
from jax import lax
from jax.experimental import pallas as pl
from jax.experimental.pallas import tpu as pltpu
from jax.sharding import Mesh
from jax.sharding import PartitionSpec as P

HQ = 32
HK = 8
HEAD = 64

EPS = 1e-05
BASE = 500000.0
MASKED = -1e30

BF = jnp.bfloat16
F32 = jnp.float32


def positions_of(lengths, index):
    ends = jnp.cumsum(lengths)
    starts = ends - lengths
    segment = jnp.sum((index[:, None] >= ends[None, :-1]).astype(jnp.int32), axis=1)
    member = segment[:, None] == jnp.arange(lengths.shape[0], dtype=jnp.int32)[None, :]
    start = jnp.sum(jnp.where(member, starts[None, :], 0), axis=1)
    place = jnp.where(segment == 0, index, lengths[0] + index - start)
    return (segment, place)


def matmul(left, right):
    return jnp.dot(left, right, preferred_element_type=F32)


def contract_last(left, right):
    return lax.dot_general(left, right, (((1,), (1,)), ((), ())), preferred_element_type=F32)


def contract_first(left, right):
    return lax.dot_general(left, right, (((0,), (0,)), ((), ())), preferred_element_type=F32)


def norm_back(grad_normed, unit, inverse, gain):
    scaled = grad_normed * gain
    return inverse * (scaled - unit * jnp.mean(scaled * unit, axis=1, keepdims=True))


def after(value, *others):
    return lax.optimization_barrier((value,) + others)[0]


def after(value, *others):
    return lax.optimization_barrier((value,) + others)[0]


def step_to(value, axis, step):
    size = lax.axis_size(axis)
    return lax.ppermute(value, axis, [(i, i ^ step) for i in range(size)])


def exchange(blocks):
    return lax.all_to_all(blocks, "group", 0, 0, tiled=True)


def spread(mine):
    parts = lax.axis_size("group")
    blocks = exchange(jnp.broadcast_to(mine[None], (parts,) + mine.shape))
    return blocks.reshape((parts * mine.shape[0],) + mine.shape[1:])


def from_core(value):
    return step_to(value, "core", 1)


def with_core(got):
    if lax.axis_size("core") == 1:
        return got
    return jnp.concatenate([got, from_core(got)], axis=0)


def scatter_send(partial):
    parts = lax.axis_size("group")
    if lax.axis_size("core") == 2:
        half = partial.shape[0] // 2
        partial = partial[:half] + from_core(partial[half:].astype(BF)).astype(F32)
    rows = partial.shape[0] // parts
    return partial.astype(BF).reshape((parts, rows) + partial.shape[1:])


def scatter_sum(blocks):
    return jnp.sum(exchange(blocks).astype(F32), axis=0)


def rotated(value, cosine, sine, back):
    wide = value.shape[1]
    half = HEAD // 2
    lane = lax.broadcasted_iota(jnp.int32, value.shape, 1)
    low = lane % HEAD < half
    other = jnp.where(
        low, pltpu.roll(value, wide - half, 1), pltpu.roll(value, half, 1)
    )
    sign = jnp.where(low, -1.0, 1.0)
    if back:
        sign = -sign
    return value * cosine + other * sign * sine


def visible(place_query, segment_query, place_key, segment_key):
    same = (segment_key == 0) | (segment_key == segment_query)
    return same & (place_key <= place_query)


def forward_kernel(qkv_ref, cos_ref, sin_ref, column_ref, row_ref, o_ref, kept_ref, lse_ref):
    heads = HQ // HK
    wide = heads * HEAD
    scale = HEAD ** (-0.5)
    cosine, sine = cos_ref[...], sin_ref[...]
    tiles = wide // cosine.shape[1]
    query = rotated(
        qkv_ref[:, :wide],
        jnp.concatenate([cosine] * tiles, axis=1),
        jnp.concatenate([sine] * tiles, axis=1),
        False,
    )
    query = query.astype(BF)
    pair = qkv_ref[:, wide:]
    lane = lax.broadcasted_iota(jnp.int32, pair.shape, 1)
    pair = jnp.where(lane < HEAD, rotated(pair, cosine, sine, False), pair).astype(BF)
    kept_ref[:, :wide] = query
    kept_ref[:, wide:] = pair
    key, value = pair[:, :HEAD], pair[:, HEAD:]
    allowed = visible(column_ref[:, 0:1], column_ref[:, 1:2], row_ref[0:1, :], row_ref[1:2, :])
    found = []
    for h in range(heads):
        one = query[:, h * HEAD : (h + 1) * HEAD]
        scores = jnp.where(allowed, contract_last(one, key) * scale, MASKED)
        top = jnp.max(scores, axis=1, keepdims=True)
        expo = jnp.exp(scores - top)
        denom = jnp.sum(expo, axis=1, keepdims=True)
        probs = (expo / denom).astype(BF)
        o_ref[:, h * HEAD : (h + 1) * HEAD] = matmul(probs, value).astype(BF)
        found.append(top + jnp.log(denom))
    place = lax.broadcasted_iota(jnp.int32, lse_ref.shape, 1)
    total = jnp.zeros(lse_ref.shape, F32)
    for h in range(heads):
        total = jnp.where(place == h, found[h], total)
    lse_ref[...] = total


def backward_kernel(
    kept_ref, lse_ref, grad_ref, cos_ref, sin_ref, column_ref, row_ref, out_ref, hold_ref
):
    heads = HQ // HK
    wide = heads * HEAD
    scale = HEAD ** (-0.5)
    key = kept_ref[:, wide : wide + HEAD]
    value = kept_ref[:, wide + HEAD :]
    allowed = visible(column_ref[:, 0:1], column_ref[:, 1:2], row_ref[0:1, :], row_ref[1:2, :])
    total = key.shape[0]
    grad_k = jnp.zeros((total, HEAD), F32)
    grad_v = jnp.zeros((total, HEAD), F32)
    for h in range(heads):
        one = kept_ref[:, h * HEAD : (h + 1) * HEAD]
        grad = grad_ref[:, h * HEAD : (h + 1) * HEAD]
        scores = jnp.where(allowed, contract_last(one, key) * scale, MASKED)
        probs = jnp.exp(scores - lse_ref[:, h : h + 1])
        grad_p = contract_last(grad, value)
        grad_s = probs * (grad_p - jnp.sum(probs * grad_p, axis=1, keepdims=True))
        grad_s = grad_s.astype(BF)
        hold_ref[:, h * HEAD : (h + 1) * HEAD] = matmul(grad_s, key) * scale
        grad_k = grad_k + contract_first(grad_s, one)
        grad_v = grad_v + contract_first(probs.astype(BF), grad)
    hold_ref[:, wide : wide + HEAD] = grad_k * scale
    hold_ref[:, wide + HEAD :] = grad_v
    cosine, sine = cos_ref[...], sin_ref[...]
    tiles = wide // cosine.shape[1]
    out_ref[:, :wide] = rotated(
        hold_ref[:, :wide],
        jnp.concatenate([cosine] * tiles, axis=1),
        jnp.concatenate([sine] * tiles, axis=1),
        True,
    ).astype(BF)
    pair = hold_ref[:, wide:]
    lane = lax.broadcasted_iota(jnp.int32, pair.shape, 1)
    pair = jnp.where(lane < HEAD, rotated(pair, cosine, sine, True), pair)
    out_ref[:, wide:] = pair.astype(BF)


def by_group(kernel, total, groups, inputs, outputs, scratch=()):
    def spec(shape):
        if len(shape) == 3:
            return pl.BlockSpec((None,) + shape[1:], lambda i: (i, 0, 0))
        return pl.BlockSpec((total, shape[1]), lambda i: (i, 0))

    return pl.pallas_call(
        kernel,
        grid=(groups,),
        in_specs=[spec(one.shape) for one in inputs],
        out_specs=[spec(one.shape) for one in outputs],
        out_shape=list(outputs),
        scratch_shapes=list(scratch),
        compiler_params=pltpu.CompilerParams(vmem_limit_bytes=40 * 2**20),
        cost_estimate=pl.CostEstimate(flops=0, bytes_accessed=1, transcendentals=0),
    )(*inputs)


class Clock:
    def __init__(self):
        self.token = jnp.zeros((8, 128), F32)

    def tick(self, *values):
        flat, tree = jax.tree.flatten(values)
        out = lax.optimization_barrier((self.token, *flat))
        self.token = out[0]
        values = jax.tree.unflatten(tree, out[1:])
        return values[0] if len(values) == 1 else values

    def now(self, value):
        return after(value, self.token)


class Line:
    def __init__(self, clock, shape):
        self.clock = clock
        self.shape = shape
        place = lax.axis_index("rest")
        self.inner = (place == 1) | (place == 2)
        self.sums = {}
        self.flight = {}

    def piece(self, array, block):
        rows, wide = self.shape
        if array.ndim == 3:
            return array[block[0]]
        row, column = block
        return array[row * rows : (row + 1) * rows, column * wide : (column + 1) * wide]

    def slot(self, entering, *values):
        last = self.flight
        came, moved, values = self.clock.tick(last.get("came"), last.get("moved"), values)
        if entering is not None:
            name, array, block = entering
            entering = (name, self.clock.now(array), block)
        part, send = self.combine(last, came, moved, entering)
        across = last["enter"][0] if part is not None else None
        flight = {"enter": entering, "across": across, "part": part}
        if last.get("across"):
            flight["out"] = (last["across"], send)
        if part is not None:
            flight["moved"] = lax.ppermute(part, "rest", [(1, 2), (2, 1)])
        if send is not None:
            flight["came"] = lax.ppermute(send, "rest", [(0, 1), (1, 0), (2, 3), (3, 2)])
        if last.get("out"):
            name, full = last["out"]
            self.sums[name] = (full, came)
        self.flight = flight
        return values[0] if len(values) == 1 else values

    def stack(self, name, count):
        rows, wide = self.shape
        steps = 2
        tile = rows // steps
        pairs = [self.sums[name, k] for k in range(count)]

        def spec(k, used):
            def at(j, i, w):
                here = jnp.where(j == k, i, jnp.where(j < k, 0, steps - 1))
                return (jnp.where(w[0] == used, here, 0), 0)

            return pl.BlockSpec((tile, wide), at)

        def kernel(where_ref, *refs):
            for k in range(count):
                for used in range(2):

                    @pl.when((pl.program_id(0) == k) & (where_ref[0] == used))
                    def _(k=k, used=used):
                        refs[-1][...] = refs[2 * k + 1 - used][...]

        return pl.pallas_call(
            kernel,
            grid_spec=pltpu.PrefetchScalarGridSpec(
                num_scalar_prefetch=1,
                grid=(count, steps),
                in_specs=[spec(k, used) for k in range(count) for used in (1, 0)],
                out_specs=pl.BlockSpec((None, tile, wide), lambda j, i, w: (j, i, 0)),
            ),
            out_shape=jax.ShapeDtypeStruct((count, rows, wide), BF),
            compiler_params=pltpu.CompilerParams(vmem_limit_bytes=16 * 2**20),
            cost_estimate=pl.CostEstimate(flops=0, bytes_accessed=1, transcendentals=0),
        )(self.inner.astype(jnp.int32)[None], *[one for pair in pairs for one in pair])

    def combine(self, stream, came, moved, entering):
        rows, wide = self.shape
        steps = 2
        tile = rows // steps
        last, across = stream.get("enter"), stream.get("across")

        def spec(block, used):
            def at(i, w):
                here = jnp.where(w[0] == used, i, 0)
                return block[:-2] + (block[-2] * steps + here, block[-1])

            return pl.BlockSpec((None,) * (len(block) - 2) + (tile, wide), at)

        inputs, names = [], []

        def take(name, array, block, used):
            if name == "last":
                array = pltpu.with_memory_space_constraint(array, pltpu.HBM)
            inputs.append((array, spec(block, used)))
            names.append(name)

        if last is not None:
            take("came", came, (0, 0), 1)
            take("last", last[1], last[2], 1)
        if across is not None:
            take("part", stream["part"], (0, 0), 1)
            take("moved", moved, (0, 0), 1)
        if entering is not None:
            take("next", entering[1], entering[2], 0)
        given = []
        if last is not None:
            given.append("part")
        if across is not None or entering is not None:
            given.append("send")
        if not given:
            return None, None

        def kernel(where_ref, *refs):
            read = dict(zip(names, refs))
            write = dict(zip(given, refs[len(names) :]))

            @pl.when(where_ref[0] == 1)
            def _():
                if "last" in read:
                    total = read["last"][...].astype(F32) + read["came"][...].astype(F32)
                    write["part"][...] = total.astype(BF)
                if "part" in read:
                    total = read["part"][...].astype(F32) + read["moved"][...].astype(F32)
                    write["send"][...] = total.astype(BF)

            if "next" in read:

                @pl.when(where_ref[0] == 0)
                def _():
                    write["send"][...] = read["next"][...]

        results = pl.pallas_call(
            kernel,
            grid_spec=pltpu.PrefetchScalarGridSpec(
                num_scalar_prefetch=1,
                grid=(steps,),
                in_specs=[one[1] for one in inputs],
                out_specs=[
                    pl.BlockSpec(
                        (tile, wide),
                        lambda i, w: (i, 0)
                        if name == "send"
                        else (jnp.where(w[0] == 1, i, 0), 0),
                    )
                    for name in given
                ],
            ),
            out_shape=[jax.ShapeDtypeStruct((rows, wide), BF)] * len(given),
            compiler_params=pltpu.CompilerParams(vmem_limit_bytes=16 * 2**20),
            cost_estimate=pl.CostEstimate(flops=0, bytes_accessed=1, transcendentals=0),
        )(self.inner.astype(jnp.int32)[None], *[one[0] for one in inputs])
        results = dict(zip(given, results))
        return results.get("part"), results.get("send")


def place(shape, mine, other, rows, wide, blocks):
    core = lax.axis_index("core")
    table = jnp.asarray(
        [[list(there) + list(here(k)) for k in range(2)] for there, here in blocks], jnp.int32
    )
    table = jnp.stack([table[:, 0], table[:, 1]])
    table = jnp.where(core == 0, table, table[::-1])
    count = len(blocks)
    table = table.reshape(-1)
    size = table.shape[0] // (2 * count)

    def entry(w, k, j, field):
        return w[(k * count + j) * size + field]

    def source(k, j, w, own):
        j = jnp.where(k == own, j, count - 1 if own == 0 else 0)
        return tuple(entry(w, k, j, field) for field in range(3))

    def kernel(table_ref, mine_ref, other_ref, out_ref):
        @pl.when(pl.program_id(0) == 0)
        def _():
            out_ref[...] = mine_ref[...].astype(F32)

        @pl.when(pl.program_id(0) == 1)
        def _():
            out_ref[...] = other_ref[...].astype(F32)

    return pl.pallas_call(
        kernel,
        grid_spec=pltpu.PrefetchScalarGridSpec(
            num_scalar_prefetch=1,
            grid=(2, count),
            in_specs=[
                pl.BlockSpec((None, rows, wide), lambda k, j, w: source(k, j, w, 0)),
                pl.BlockSpec((None, rows, wide), lambda k, j, w: source(k, j, w, 1)),
            ],
            out_specs=pl.BlockSpec(
                (rows, wide), lambda k, j, w: (entry(w, k, j, 3), entry(w, k, j, 4))
            ),
        ),
        out_shape=jax.ShapeDtypeStruct(shape, F32),
        compiler_params=pltpu.CompilerParams(vmem_limit_bytes=16 * 2**20),
        cost_estimate=pl.CostEstimate(
            flops=0, bytes_accessed=12 * count * rows * wide, transcendentals=0
        ),
    )(table, mine, other)


def body(
    tokens,
    seq_lengths,
    attn_gain,
    w_query,
    w_key,
    w_value,
    w_out,
    mlp_gain,
    w_gate,
    w_up,
    w_down,
    cotangent,
):
    parts = lax.axis_size("group")
    cores = lax.axis_size("core")
    g = lax.axis_index("group")
    c = lax.axis_index("core")
    rows, width = tokens.shape[1:]
    total = rows * parts
    team = parts * cores
    heads = HQ // HK
    scale = HEAD ** (-0.5)
    ff = w_gate.shape[1] // team
    share = w_gate.shape[0]
    qw = HQ * HEAD // team
    kw = HK * HEAD // team
    assert kw == HEAD

    def columns(weight, size, rows=slice(None)):
        return jnp.stack(
            [
                lax.dynamic_slice_in_dim(weight[rows], (k * cores + c) * size, size, 1)
                for k in range(parts)
            ]
        )

    def fetch(blocks):
        return [
            step_to(lax.dynamic_index_in_dim(blocks, g ^ s, 0, keepdims=False), "group", s)
            for s in range(1, parts)
        ]

    def in_order(own, got):
        out = jnp.zeros((parts,) + own.shape, own.dtype)
        for s, block in enumerate([own] + got):
            out = lax.dynamic_update_slice_in_dim(out, block[None], g ^ s, 0)
        return out.reshape((parts * own.shape[0],) + own.shape[1:])

    def own_columns(weight, size):
        return lax.dynamic_slice_in_dim(weight, (g * cores + c) * size, size, 1)

    clock = Clock()
    x_mine = tokens[0]
    extra = 2 * share // width if 2 * share > width else 1
    gains = jnp.concatenate([attn_gain, mlp_gain])
    gains = jnp.pad(gains, (0, 16 * width - gains.shape[0])).reshape(16, width)
    x_got = spread(jnp.concatenate([x_mine, gains], axis=0))
    x_got = x_got.reshape(parts, rows + 16, width)
    gains = x_got[:, rows].reshape(parts, width)[:, : 2 * share]
    gain_one = gains[:, :share].reshape(-1).astype(F32)
    gain_two = gains[:, share:].reshape(-1).astype(F32)
    x_got = x_got[:, :rows].reshape(parts * rows, width)
    qkv_send = jnp.concatenate(
        [columns(w_query, qw), columns(w_key, kw), columns(w_value, kw)], axis=2
    )
    qkv_got = fetch(qkv_send)
    qkv_own = lax.dynamic_index_in_dim(qkv_send, g, 0, keepdims=False)

    paired = lax.axis_size("rest") == 4
    even = lax.axis_index("rest") % 2 == 0
    halves = [slice(0, share // 4 * 3), slice(share // 4 * 3, share)]
    sends = []
    for half in halves:
        gate_send = columns(w_gate, ff, half)
        up_send = columns(w_up, ff, half)
        sends.append([jnp.where(even, gate_send, up_send)] if paired else [gate_send, up_send])
    lengths = [seq_lengths[0]]
    if cores == 2:
        lengths.append(from_core(seq_lengths[0]))
    index = jnp.arange(total, dtype=jnp.int32)
    marks = [positions_of(one, index) for one in lengths]
    half = HEAD // 2
    freq = BASE ** (-(2.0 * jnp.arange(half, dtype=F32)) / HEAD)
    place_all = jnp.concatenate([one[1] for one in marks]).astype(F32)
    angle = place_all[:, None] * jnp.tile(freq, 128 // half)[None, :]
    cosine, sine = jnp.cos(angle), jnp.sin(angle)
    marks_row = jnp.stack([jnp.stack([one[1], one[0]]) for one in marks])
    marks_column = marks_row.transpose(0, 2, 1)
    x_got, qkv_got, sends, cosine, sine, marks_row, marks_column = clock.tick(
        x_got, qkv_got, sends, cosine, sine, marks_row, marks_column
    )

    out_rows = lax.dynamic_slice_in_dim(w_out, c * qw, qw, 0)
    down_rows = lax.dynamic_slice_in_dim(w_down, c * ff, ff, 0)
    first_got = [[fetch(one) for one in sends[0]]]
    second_got = []
    qkv_full = in_order(qkv_own, qkv_got)
    x_all = with_core(x_got)

    def swap(got):
        return step_to(jnp.stack(got[0]), "rest", 1)

    def fill(out, got, row):
        for s in range(1, parts):
            out = lax.dynamic_update_slice(out, got[s - 1][None], (g ^ s, row, 0))
        return out

    def begin(own):
        return lax.dynamic_update_slice_in_dim(
            jnp.zeros((parts, share, ff), BF), own[None], g, 0
        )

    def ordered(first, second):
        if not paired:
            return first, second
        return jnp.where(even, first, second), jnp.where(even, second, first)

    x = x_all.astype(F32)
    inverse_all = lax.rsqrt(jnp.mean(x * x, axis=1, keepdims=True) + EPS)
    normed_one = (x * inverse_all * gain_one).astype(BF)
    qkv = matmul(normed_one, qkv_full)
    attended, kept, logsum = by_group(
        forward_kernel,
        total,
        cores,
        [qkv, cosine, sine, marks_column, marks_row],
        [
            jax.ShapeDtypeStruct((cores * total, qw), BF),
            jax.ShapeDtypeStruct((cores * total, qw + 2 * kw), BF),
            jax.ShapeDtypeStruct((cores * total, 128), F32),
        ],
    )
    x_own = x_mine.astype(F32)
    send = scatter_send(matmul(attended, out_rows))
    send, first_got, kept, attended, logsum = clock.tick(
        send, first_got, kept, attended, logsum
    )

    if paired:
        second_got.append(swap(first_got[0]))
    first_got.append([fetch(clock.now(one)) for one in sends[1]])
    own = [own_columns(w_gate, ff), own_columns(w_up, ff)]
    if paired:
        own = ordered(*own)
    first_full = fill(begin(clock.now(own[0])), first_got[0][0], 0)
    second_full = begin(clock.now(own[1]))
    mid = x_own + scatter_sum(send)
    mid, first_got, first_full, second_full = clock.tick(
        mid, first_got, first_full, second_full
    )

    inverse_two = lax.rsqrt(jnp.mean(mid * mid, axis=1, keepdims=True) + EPS)
    unit_two = mid * inverse_two
    if paired:
        second_got.append(swap(first_got[1]))
    normed_two = spread((unit_two * gain_two).astype(BF))
    cot_all = spread(clock.now(cotangent[0]))
    split = share // 4 * 3
    first_full = fill(first_full, first_got[1][0], split)
    others = second_got if paired else [got[1] for got in first_got]
    second_full = fill(second_full, others[0], 0)
    normed_two, second_got, unit_two, inverse_two, first_full, second_full = clock.tick(
        normed_two, second_got, unit_two, inverse_two, first_full, second_full
    )
    normed_two = with_core(normed_two)
    cot_all = with_core(cot_all)
    others = second_got if paired else [got[1] for got in first_got]
    second_full = fill(second_full, others[1], split)
    first_full = first_full.reshape(share * parts, ff)
    second_full = second_full.reshape(share * parts, ff)
    gate, up = ordered(matmul(normed_two, first_full), matmul(normed_two, second_full))
    sigma = jax.nn.sigmoid(gate)
    active = (gate * sigma * up).astype(BF)
    grad_down = contract_first(active, cot_all).astype(BF)
    on_line = paired and cores == 2
    line = Line(clock, (share, ff))
    outs = {}

    def slot(entering, *values):
        if on_line:
            return line.slot(entering, *values)
        return clock.tick(*values) if values else None

    active, cot_all, grad_down = slot(
        (("down", 0), grad_down, (0, 0)), active, cot_all, grad_down
    )
    grad_active = contract_last(cot_all, down_rows)
    grad_gate_pre = (grad_active * up * sigma * (1.0 + gate * (1.0 - sigma))).astype(BF)
    grad_up_pre = (grad_active * gate * sigma).astype(BF)
    first_pre, second_pre = ordered(grad_gate_pre, grad_up_pre)
    partial = contract_last(first_pre, first_full) + contract_last(second_pre, second_full)
    grad_gate_pre, grad_up_pre, partial = slot(
        (("down", 1), grad_down, (0, 1)), grad_gate_pre, grad_up_pre, partial
    )
    grad_normed_two = scatter_sum(scatter_send(partial))
    grad_gate = contract_first(normed_two, grad_gate_pre).astype(BF)
    grad_gate = clock.tick(grad_gate) if not on_line else grad_gate
    slot((("gate", 0), grad_gate, (0, 0)))
    grad_up = contract_first(normed_two, clock.now(grad_up_pre)).astype(BF)
    grad_up, grad_normed_two = slot((("gate", 1), grad_gate, (1, 0)), grad_up, grad_normed_two)
    grad_y = cotangent[0].astype(F32)
    grad_gain_two = jnp.sum(grad_normed_two * unit_two, axis=0)
    grad_mid = grad_y + norm_back(grad_normed_two, unit_two, inverse_two, gain_two)
    grad_branch = spread(grad_mid.astype(BF))
    grad_mid, grad_gain_two, grad_branch = slot(
        (("gate", 2), grad_gate, (2, 0)), grad_mid, grad_gain_two, grad_branch
    )
    grad_branch = with_core(grad_branch)
    grad_attended = contract_last(grad_branch, out_rows).astype(BF)
    grad_out = contract_first(attended, grad_branch).astype(BF)
    grad_attended, grad_out = slot(
        (("gate", 3), grad_gate, (3, 0)), grad_attended, grad_out
    )

    def both(mine):
        mine = clock.now(mine)
        return mine, from_core(mine)

    (grad_qkv,) = by_group(
        backward_kernel,
        total,
        cores,
        [kept, logsum, grad_attended, cosine, sine, marks_column, marks_row],
        [jax.ShapeDtypeStruct((cores * total, qw + 2 * kw), BF)],
        [pltpu.VMEM((total, qw + 2 * kw), F32)],
    )
    grad_qkv = slot((("up", 0), grad_up, (0, 0)), grad_qkv)
    grad_weights = contract_first(normed_one, grad_qkv).astype(BF)
    send = scatter_send(contract_last(grad_qkv, qkv_full))
    grad_weights, send = slot((("up", 1), grad_up, (1, 0)), grad_weights, send)
    grad_normed_one = scatter_sum(send)
    grad_normed_one = slot((("up", 2), grad_up, (2, 0)), grad_normed_one)
    inverse_one = lax.rsqrt(jnp.mean(x_own * x_own, axis=1, keepdims=True) + EPS)
    unit_one = x_own * inverse_one
    grad_gain_one = jnp.sum(grad_normed_one * unit_one, axis=0)
    grad_x = grad_mid + norm_back(grad_normed_one, unit_one, inverse_one, gain_one)
    each = qw + 2 * kw
    grad_gains = jnp.stack([grad_gain_one, grad_gain_two]).reshape(2, parts, share)
    grad_gains = grad_gains.transpose(1, 0, 2).reshape(parts, 2 * share).astype(BF)
    grad_gains = jnp.pad(grad_gains, ((0, 0), (0, 16 * each - 2 * share)))
    turned = exchange(
        jnp.concatenate(
            [grad_weights.reshape(parts, share, each), grad_gains.reshape(parts, 16, each)],
            axis=1,
        )
    )
    turned, grad_x = slot((("up", 3), grad_up, (3, 0)), turned, grad_x)
    grad_gains = turned[:, share:].reshape(parts, 16 * each)[:, : 2 * share]
    grad_gains = jnp.sum(grad_gains.reshape(parts, 2, share).astype(F32), axis=0)
    turned = turned[:, :share]
    turned_q = turned[:, :, :qw].transpose(1, 0, 2).reshape(share, parts * qw)
    turned_kv = turned[:, :, qw:].transpose(1, 0, 2).reshape(share, parts * 2 * kw)
    if on_line:
        turned_kv = jnp.concatenate(
            [
                turned_kv,
                jnp.pad(
                    grad_gains.astype(BF), ((0, share - 2), (0, ff - parts * 2 * kw - share))
                ),
            ],
            axis=1,
        )

        def turn(name):
            return exchange(line.stack(name, parts))

        def place_columns(turned):
            return place(
                (share, ff * team),
                *both(turned),
                share,
                ff,
                [((j, 0, 0), lambda k, j=j: (0, j * 2 + k)) for j in range(parts)],
            )

        gate_turned = turn("gate")
        grad_out = jnp.concatenate([grad_out[:, :ff], grad_out[:, ff:]], axis=0)
        turned_q, turned_kv, grad_out = slot(
            (("down", 2), grad_down, (1, 0)), turned_q, turned_kv, grad_out
        )
        result = matmul(clock.now(active), down_rows)
        gate_turned, result = slot(
            (("down", 3), grad_down, (1, 1)), gate_turned, result
        )
        outs["gate"] = place_columns(gate_turned)
        outs = slot((("heads", 0), turned_q, (0, 0)), outs)
        up_turned = turn("up")
        slot((("heads", 1), turned_kv, (0, 0)))
        result = scatter_send(clock.now(result))
        up_turned, result = slot((("rows", 0), grad_out, (0, 0)), up_turned, result)
        outs["up"] = place_columns(up_turned)
        result = mid + scatter_sum(result)
        outs, result = slot(None, outs, result)
        outs["down"] = place(
            (ff * 2, width),
            *both(line.stack("down", 4)),
            share,
            ff,
            [
                ((a * 2 + b, 0, 0), lambda k, a=a, b=b: (k * 2 + a, b))
                for a in range(2)
                for b in range(2)
            ],
        )
        outs = slot(None, outs)
        mine, other = both(line.stack("heads", 2))
        grad_gains = sum(
            one[1, :2, parts * 2 * kw : parts * 2 * kw + share].astype(F32) for one in (mine, other)
        )
        outs["query"] = place(
            (share, qw * team),
            mine,
            other,
            share,
            qw,
            [((0, 0, j), lambda k, j=j: (0, j * 2 + k)) for j in range(parts)],
        )
        narrow = [
            one[1, :, : parts * 2 * kw].reshape(share, parts, 2 * kw) for one in (mine, other)
        ]
        narrow = jnp.stack(
            [jnp.where(c == 0, *narrow), jnp.where(c == 0, *narrow[::-1])], axis=2
        ).astype(F32)
        outs["key"] = narrow[..., :kw].reshape(share, team * kw)
        outs["value"] = narrow[..., kw:].reshape(share, team * kw)
        outs = slot(None, outs)
        outs["out"] = place(
            (qw * 2, width),
            *both(line.stack("rows", 1)),
            qw,
            ff,
            [((0, b, 0), lambda k, b=b: (k, b)) for b in range(2)],
        )
    else:
        result = mid + scatter_sum(scatter_send(matmul(active, down_rows)))

        def whole(value):
            value = lax.psum(value, "rest")[None]
            if cores == 2:
                other = from_core(value)
                value = jnp.concatenate(
                    [jnp.where(c == 0, value, other), jnp.where(c == 0, other, value)]
                )
            return value.astype(F32)

        def beside(value):
            return value.transpose(2, 1, 0, 3).reshape(share, -1)

        grad_gains = lax.psum(grad_gains, ("rest", "core"))
        outs["down"] = whole(grad_down).reshape(cores * ff, width)
        outs["out"] = whole(grad_out).reshape(cores * qw, width)
        for name, grad in (("gate", grad_gate), ("up", grad_up)):
            outs[name] = beside(whole(exchange(grad.reshape(parts, share, ff))))
        turned = whole(turned)
        outs["query"] = beside(turned[..., :qw])
        outs["key"] = beside(turned[..., qw : qw + kw])
        outs["value"] = beside(turned[..., qw + kw :])
    return (
        result.astype(BF)[None],
        grad_x.astype(BF)[None],
        grad_gains[0],
        outs["query"],
        outs["key"],
        outs["value"],
        outs["out"],
        grad_gains[1],
        outs["gate"],
        outs["up"],
        outs["down"],
    )


def solution(mesh):
    parts, replicas = mesh.devices.shape
    cores = 2 if HK % (2 * parts) == 0 and replicas % 2 == 0 else 1
    split = Mesh(
        mesh.devices.reshape(parts, replicas // cores, cores), ("group", "rest", "core")
    )
    replica = ("rest", "core")
    weights = (P("group"),) + (P("group", None),) * 4 + (P("group"),) + (P("group", None),) * 3
    split_tokens = P(replica, "group", None)
    return jax.shard_map(
        body,
        mesh=split,
        in_specs=(split_tokens, P(replica, None)) + weights + (split_tokens,),
        out_specs=(split_tokens, split_tokens) + weights,
        check_vma=False,
    )
```
